128 devices in a mesh: enc: 16 (over z, y), dom: 8 (over x, core).
Axes of the slice: x: 4, y: 4, z: 4, core: 2. Of those that a mesh axis runs over, the one named last changes fastest.
Arguments:
- token_states: bfloat16 [131072, 1024], P(('enc', 'dom')), may hold values from -6 to 6
- token_nodes: int32 [128, 1024], P(('enc', 'dom')), may hold values from 0 to 191, never falling along the last dimension, each value on 1 to 21 neighbouring positions
- expand_weight: bfloat16 [1024, 4096], replicated, may hold values from -0.1875 to 0.1875
- contract_weight: bfloat16 [4096, 1024], replicated, may hold values from -0.09375 to 0.09375
- node_owner: int32 [24576, 1], P(('enc', 'dom')), may hold values from 0 to 127; in each aligned block of 192 rows (0 to 191, 192 to 383, ...) at most 2 rows name the same one
- tile_columns: int32 [128, 2, 3], P(('enc', 'dom')), may hold values from 0 to 3, as said below
- tile_count: int32 [128, 2], P(('enc', 'dom')), may hold values from 1 to 3
- tile_values: bfloat16 [128, 2, 3, 128, 128], P(('enc', 'dom')), may hold values from -1.5 to 1.5
- first_weight: bfloat16 [1024, 1024], replicated, may hold values from -0.1875 to 0.1875
- second_weight: bfloat16 [1024, 1024], replicated, may hold values from -0.1875 to 0.1875
- output_cotangent: bfloat16 [32768, 1024], P(('enc', 'dom')), may hold values from -1.1953125 to 1.1953125
Outputs:
- graph_output: bfloat16 [32768, 1024], P(('enc', 'dom'))
- node_grads: bfloat16 [24576, 1024], P(('enc', 'dom'))
The draws below stay inside these ranges and needn't reach their ends.
Inputs may be any that keep to these rules, and one draw needn't show every extreme that they name: `token_nodes`: each row lists one device's 1024 tokens by node, in order: node numbers never fall and each of the 192 nodes has 1 to 21 tokens. `node_owner`: among the nodes of one device, at most 2 have the same owner. `tile_columns`: the entries of row tile r are distinct and lie among r, r + 1 and r + 2; column tile 0 is the left owner's last 128 slots, the tiles after it are the owner's own, and the last column tile, one past the owner's own, is the right owner's first 128 slots. Only the first tile_count entries are used.
All inputs are finite; a program needn't handle non-finite values.
Results may differ from the reference program's by a relative error of at most 0.014.
Values may be sent and summed in bfloat16 or wider, within the bound.
No kernel may reach another device: no remote copies, remote signals or barrier semaphores. Data moves between devices by JAX's collectives and lax.ppermute only.
A program may use at most 128 MiB of HBM per device.

```python
import math
import jax
import jax.numpy as jnp
import numpy as np
from jax import lax

D = 1024
FF = 4096
TOK_DEV = 1024
NODE_DEV = 192
SLOTS = 256
TILE = 128
TILE_SLOTS = 3
ROW_TILES = 2
CAP = 2
MOST_LEN = 21
TOKENS = 131072
NODES = 24576
VERTS = 32768
N_ENC = 16
N_DOM = 8
DEVICES = 128


def draw_tile_count(key, part):
    key = jax.random.fold_in(key, 31)
    counted = jax.random.randint(key, (N_ENC * N_DOM, ROW_TILES), 1, TILE_SLOTS + 1)
    counted = counted.at[0, 0].set(TILE_SLOTS)
    counted = counted.at[0, 1].set(1)
    return counted.astype(jnp.int32)


def draw_tile_columns(key, part):
    key = jax.random.fold_in(key, 47)
    first_key, second_key = jax.random.split(key)
    offset = jax.random.randint(first_key, (N_ENC * N_DOM, ROW_TILES, 1), 0, TILE_SLOTS)
    flipped = jax.random.randint(second_key, (N_ENC * N_DOM, ROW_TILES, 1), 0, 2)
    stride = jnp.arange(TILE_SLOTS, dtype=jnp.int32)[None, None, :]
    stride = jnp.where(flipped == 1, -stride, stride)
    picked = (offset + stride) % TILE_SLOTS
    return (jnp.arange(ROW_TILES, dtype=jnp.int32)[None, :, None] + picked).astype(jnp.int32)


def block_scale(key, shape, cuts, low, top_value):
    loudness, own = 1.0, jax.random.fold_in(key, 6)
    for axis_at, parts in cuts:
        heights = jnp.exp(jax.random.uniform(jax.random.fold_in(own, axis_at), (parts,), jnp.float32, low / len(cuts), top_value / len(cuts)))
        loudness = loudness * jnp.repeat(heights, shape[axis_at] // parts).reshape([-1 if axis == axis_at else 1 for axis in range(len(shape))])
    return loudness


def split_up(amount, total, most, slope):
    loads = [(1 << 20) // math.isqrt(grade ** slope) + 1 for grade in range(2, amount + 1)]
    spare, given = total - most - (amount - 1), [1] * (amount - 1)
    while spare > 0:
        free = [i for i in range(amount - 1) if given[i] < most]
        pool, remaining = sum([loads[i] for i in free]), spare
        for i in free:
            extra = min(most - given[i], max(1, remaining * loads[i] // pool), spare)
            given[i] = given[i] + extra
            spare = spare - extra
    return np.array([most] + given)


def uneven_parts(stream_key, amount, total, reach, lean):
    if amount == 2:
        one = jax.random.randint(stream_key, (), max(1, total - reach), min(reach, total - 1) + 1)
        return jnp.stack([one, total - one])
    lengths = jnp.asarray(split_up(amount, total, reach, lean), jnp.int32)
    twos = (amount - 1) // 2
    source_of, sink = lengths[1:1 + 2 * twos:2], lengths[2:2 + 2 * twos:2]
    slack = jnp.minimum(source_of - 1, reach - sink)
    passed = jax.random.randint(jax.random.fold_in(stream_key, 1), (twos,), 0, 1 << 20) % (slack + 1)
    lengths = lengths.at[1:1 + 2 * twos:2].set(source_of - passed).at[2:2 + 2 * twos:2].set(sink + passed)
    return lengths[jax.random.permutation(jax.random.fold_in(stream_key, 2), amount)]


def routed_block(stream_key, own, number, rows, count, top, reach, skew):
    order = jax.random.permutation(stream_key, count)
    packed, usual = portions_of(count, rows * top, reach, skew, True), portions_of(count, rows * top, reach, skew, False)
    places = jnp.arange(count)

    def named(sizes, rotation):
        used = int((sizes > 0).sum())
        fixed = max(1, used // 4)
        shifted = fixed + (places - fixed + rotation * (used - fixed)) % max(1, count - fixed)
        return jnp.zeros((count,), jnp.int32).at[order[jnp.where(places < fixed, places, shifted)]].set(jnp.asarray(sizes, jnp.int32))

    sizes = jnp.where(number % 4 == 0, named(packed, number // 4), named(usual, number - number // 4 - 1))
    mixed = jax.random.permutation(jax.random.fold_in(own, 3), count)
    donor, receiver = mixed[0:count // 2 * 2:2], mixed[1:count // 2 * 2:2]
    slack = jnp.minimum(sizes[donor] - 1, reach - sizes[receiver]) // 2
    slack = jnp.where((donor == order[0]) | (receiver == order[0]) | (sizes[receiver] == 0), 0, jnp.maximum(slack, 0))
    shifted = jax.random.randint(jax.random.fold_in(own, 4), (count // 2,), 0, 1 << 20) % (slack + 1)
    sizes = sizes.at[donor].add(-shifted).at[receiver].add(shifted)
    members = jnp.searchsorted(jnp.cumsum(sizes), jnp.arange(rows * top), side="right").astype(jnp.int32)
    listing = members.reshape(top, rows).T
    listing = listing[jax.random.permutation(jax.random.fold_in(own, 1), rows)]
    rotation = jax.random.randint(jax.random.fold_in(own, 2), (rows, 1), 0, top)
    return jnp.take_along_axis(listing, (jnp.arange(top)[None, :] + rotation) % top, axis=1)


def portions_of(amount, total, bound, lean, full):
    weights = [(1 << 20) // math.isqrt(standing ** lean) + 1 for standing in range(1, amount + 1)]
    largest = bound if full else min(bound, max(-(-total // amount), total * weights[0] // sum(weights)))
    least = 1 if total - largest >= amount - 1 else 0
    given, surplus = [largest] + [least] * (amount - 1), total - largest - least * (amount - 1)
    while surplus > 0:
        movable = [i for i in range(1, amount) if given[i] < largest] or [i for i in range(1, amount) if given[i] < bound]
        whole, budget = sum([weights[i] for i in movable]), surplus
        for i in movable:
            extra = min(bound - given[i], max(1, budget * weights[i] // whole), surplus)
            given[i] = given[i] + extra
            surplus = surplus - extra
    return np.array(given)


def noise(own_key, extent, width, reach, shards=(), held_as=jnp.bfloat16):
    level = block_scale(own_key, extent, shards, -0.22, 0.18) if shards else 1.0
    array = jax.random.normal(own_key, extent, jnp.float32) * width * level
    return jnp.minimum(jnp.maximum(array, -reach), reach).astype(held_as)


def setup_inputs(seed: int = 0) -> dict:
    key_of = jax.random.split(jax.random.key(seed), 12)
    token_states = noise(key_of[0], (TOKENS, D), 1.0, 6.0, ((0, 128),))
    token_nodes = jax.vmap(lambda own: jnp.searchsorted(jnp.cumsum(uneven_parts(own, NODE_DEV, TOK_DEV, MOST_LEN, 2)), jnp.arange(TOK_DEV), side="right"))(jax.random.split(key_of[1], DEVICES)).reshape((DEVICES, TOK_DEV)).astype(jnp.int32)
    expand_weight = noise(key_of[2], (D, FF), D ** -0.5, 0.1875)
    contract_weight = noise(key_of[3], (FF, D), FF ** -0.5, 0.09375)
    node_owner_keys = jax.random.split(jax.random.fold_in(key_of[4], 1), NODES // NODE_DEV)
    node_owner_turns = jax.random.permutation(jax.random.fold_in(key_of[4], 3), NODES // NODE_DEV)
    node_owner = jax.vmap(lambda own, number: routed_block(jax.random.fold_in(key_of[4], 2), own, number, NODE_DEV, DEVICES, 1, CAP, 2))(node_owner_keys, node_owner_turns).reshape((NODES, 1))
    tile_columns = draw_tile_columns(jax.random.fold_in(key_of[11], 71), 0)
    tile_count = draw_tile_count(jax.random.fold_in(key_of[11], 71), 0)
    tile_values = noise(key_of[7], (DEVICES, ROW_TILES, TILE_SLOTS, TILE, TILE), 0.25, 1.5, ((0, 128),))
    first_weight = noise(key_of[8], (D, D), D ** -0.5, 0.1875)
    second_weight = noise(key_of[9], (D, D), D ** -0.5, 0.1875)
    output_cotangent = noise(key_of[10], (VERTS, D), 0.2, 1.1953125, ((0, 128),))
    return dict(token_states=token_states, token_nodes=token_nodes, expand_weight=expand_weight, contract_weight=contract_weight, node_owner=node_owner, tile_columns=tile_columns, tile_count=tile_count, tile_values=tile_values, first_weight=first_weight, second_weight=second_weight, output_cotangent=output_cotangent)


norm_eps = 1e-07

def activate(values):
    return jax.nn.gelu(values, approximate=False)

def encode(states_rows, node_ids, expand_weight, contract_weight):
    hidden = jnp.dot(states_rows, expand_weight, preferred_element_type=jnp.float32)
    hidden = activate(hidden).astype(jnp.bfloat16)
    mixed = states_rows.astype(jnp.float32) + jnp.dot(hidden, contract_weight, preferred_element_type=jnp.float32)
    average = lax.optimization_barrier(jnp.mean(mixed, axis=1, keepdims=True))
    centred = mixed - average
    variance = lax.optimization_barrier(jnp.mean(centred * centred, axis=1, keepdims=True))
    normed = (centred * lax.rsqrt(variance + norm_eps)).astype(jnp.bfloat16)
    member = node_ids[None, :] == jnp.arange(NODE_DEV, dtype=jnp.int32)[:, None]
    summed = jnp.dot(member.astype(jnp.bfloat16), normed, preferred_element_type=jnp.float32)
    counts = lax.optimization_barrier(jnp.sum(member.astype(jnp.float32), axis=1, keepdims=True))
    return (summed / counts).astype(jnp.bfloat16)

def placement(owners, capacity, slot_total):
    order = jnp.arange(owners.shape[0], dtype=jnp.int32)
    earlier = (owners[:, None] == owners[None, :]) & (order[None, :] < order[:, None])
    ranking = lax.optimization_barrier(jnp.sum(earlier.astype(jnp.int32), axis=1))
    position = (owners * capacity + ranking).astype(jnp.int32)
    return (jnp.arange(slot_total, dtype=jnp.int32)[:, None] == position[None, :]).astype(jnp.bfloat16)

def aggregate(extended, columns, counts, values):
    tile_rows = values.shape[2]
    outputs = []
    for row_tile in range(values.shape[0]):
        running = jnp.zeros((tile_rows, extended.shape[1]), jnp.float32)
        for slot_index in range(values.shape[1]):
            start = (columns[row_tile, slot_index] * tile_rows).astype(jnp.int32)
            column_block = lax.dynamic_slice_in_dim(extended, start, tile_rows, 0)
            active = (slot_index < counts[row_tile]).astype(jnp.float32)
            running = running + active * jnp.dot(values[row_tile, slot_index], column_block, preferred_element_type=jnp.float32)
        outputs.append(running)
    return jnp.concatenate(outputs, axis=0)

def spread_back(grad_rows, columns, counts, values):
    tile_rows = values.shape[2]
    row_tiles = values.shape[0]
    extended = jnp.zeros(((row_tiles + 2) * tile_rows, grad_rows.shape[1]), jnp.float32)
    for row_tile in range(row_tiles):
        grad_block = grad_rows[row_tile * tile_rows:(row_tile + 1) * tile_rows]
        for slot_index in range(values.shape[1]):
            start = (columns[row_tile, slot_index] * tile_rows).astype(jnp.int32)
            active = (slot_index < counts[row_tile]).astype(jnp.float32)
            contrib = active * lax.dot_general(values[row_tile, slot_index], grad_block, (((0,), (0,)), ((), ())), preferred_element_type=jnp.float32)
            current = lax.dynamic_slice_in_dim(extended, start, tile_rows, 0)
            extended = lax.dynamic_update_slice_in_dim(extended, current + contrib, start, 0)
    return extended

def widen(vertex_rows):
    blocks = vertex_rows.reshape(N_ENC, N_DOM, SLOTS, D)
    zeros_rim = jnp.zeros((N_ENC, 1, TILE, D), vertex_rows.dtype)
    left_rim = jnp.concatenate([zeros_rim, blocks[:, :-1, SLOTS - TILE:]], axis=1)
    right_rim = jnp.concatenate([blocks[:, 1:, :TILE], zeros_rim], axis=1)
    return jnp.concatenate([left_rim, blocks, right_rim], axis=2).reshape(N_ENC * N_DOM, SLOTS + 2 * TILE, D)

def rounded(values):
    return lax.optimization_barrier(values.astype(jnp.bfloat16)).astype(jnp.float32)

def collect(extended):
    blocks = extended.reshape(N_ENC, N_DOM, SLOTS + 2 * TILE, D)
    interior = blocks[:, :, TILE:TILE + SLOTS]
    lower_rim = rounded(blocks[:, :, :TILE])
    upper_rim = rounded(blocks[:, :, TILE + SLOTS:])
    interior = interior.at[:, 1:, :TILE].add(upper_rim[:, :-1])
    interior = interior.at[:, :-1, SLOTS - TILE:].add(lower_rim[:, 1:])
    return interior.reshape(N_ENC * N_DOM, SLOTS, D)

def mix_all(vertex_rows, tile_columns, tile_count, tile_values):
    extended = widen(vertex_rows)
    return lax.map(lambda pieces: aggregate(pieces[0], pieces[1], pieces[2], pieces[3]), (extended, tile_columns, tile_count, tile_values))

def mixback_all(grad_rows, tile_columns, tile_count, tile_values):
    spread = lax.map(lambda pieces: spread_back(pieces[0], pieces[1], pieces[2], pieces[3]), (grad_rows, tile_columns, tile_count, tile_values))
    return collect(spread)

def reference(token_states, token_nodes, expand_weight, contract_weight, node_owner, tile_columns, tile_count, tile_values, first_weight, second_weight, output_cotangent):
    devices = N_ENC * N_DOM
    capacity = SLOTS // devices
    states_rows = token_states.reshape(devices, TOK_DEV, D)
    embeds = lax.map(lambda pieces: encode(pieces[0], pieces[1], expand_weight, contract_weight), (states_rows, token_nodes))
    owners = node_owner.reshape(devices, NODE_DEV)
    onehots = lax.map(lambda owned: placement(owned, capacity, SLOTS), owners)
    outgoing = jnp.einsum('psn,pnf->psf', onehots.astype(jnp.float32), embeds.astype(jnp.float32)).astype(jnp.bfloat16)
    vertex_rows = outgoing.reshape(devices, devices, capacity, D).transpose(1, 0, 2, 3).reshape(devices, SLOTS, D)
    first_mix = mix_all(vertex_rows, tile_columns, tile_count, tile_values).astype(jnp.bfloat16)
    first_pre = jnp.dot(first_mix.reshape(devices * SLOTS, D), first_weight, preferred_element_type=jnp.float32)
    first_act = activate(first_pre).astype(jnp.bfloat16).reshape(devices, SLOTS, D)
    second_mix = mix_all(first_act, tile_columns, tile_count, tile_values).astype(jnp.bfloat16)
    graph_output = jnp.dot(second_mix.reshape(devices * SLOTS, D), second_weight, preferred_element_type=jnp.float32).astype(jnp.bfloat16)
    grad_second_mix = jnp.dot(output_cotangent, second_weight.T, preferred_element_type=jnp.float32).astype(jnp.bfloat16)
    grad_first_act = mixback_all(grad_second_mix.reshape(devices, SLOTS, D), tile_columns, tile_count, tile_values)
    derivative = jax.vjp(activate, first_pre)[1]
    grad_first_pre = derivative(grad_first_act.reshape(devices * SLOTS, D))[0].astype(jnp.bfloat16)
    grad_first_mix = jnp.dot(grad_first_pre, first_weight.T, preferred_element_type=jnp.float32).astype(jnp.bfloat16)
    grad_vertex = mixback_all(grad_first_mix.reshape(devices, SLOTS, D), tile_columns, tile_count, tile_values).astype(jnp.bfloat16)
    returned = grad_vertex.reshape(devices, devices, capacity, D).transpose(1, 0, 2, 3).reshape(devices, SLOTS, D)
    node_grads = jnp.einsum('psn,psf->pnf', onehots.astype(jnp.float32), returned.astype(jnp.float32)).astype(jnp.bfloat16)
    return (graph_output, node_grads.reshape(devices * NODE_DEV, D))
```

```python
import jax
import jax.numpy as jnp
from jax import lax
from jax.experimental import pallas as pl
from jax.experimental.pallas import tpu as pltpu
from jax.sharding import PartitionSpec as P

NODES = 192
NPAD = 256
TOKENS = 1024
D = 1024
FF = 4096
HALF = 512
PEERS = 128
GROUP = 8
ROWS = 1024
TILE = 128
SLOTS = 256

CHUNK = 512
CHUNKS = FF // CHUNK
BLOCK = 256
BLOCKS = TOKENS // BLOCK
AHEAD = 2

bf16 = jnp.bfloat16
f32 = jnp.float32
EPS = 1e-07
ROOT_HALF = 0.7071067811865476
INV_ROOT_TAU = 0.3989422804014327

ANY = pl.BlockSpec(memory_space=pl.ANY)
VMEM = pl.BlockSpec(memory_space=pltpu.VMEM)
SMEM = pl.BlockSpec(memory_space=pltpu.SMEM)


def dot(a, b):
    return jnp.dot(a, b, preferred_element_type=f32)


def dot_t(a, b):
    return lax.dot_general(a, b, (((1,), (1,)), ((), ())), preferred_element_type=f32)


def iota(shape, dim):
    return lax.broadcasted_iota(jnp.int32, shape, dim)


def params(mib):
    return pltpu.CompilerParams(vmem_limit_bytes=mib * 2**20)


def cost(flops, moved):
    return pl.CostEstimate(flops=flops, bytes_accessed=moved, transcendentals=0)


def encode_kernel(
    upper_ref,
    owner_ref,
    node_ref,
    states_hbm,
    expand_hbm,
    contract_hbm,
    out_ref,
    target_ref,
    states,
    expand,
    contract,
    total,
    hidden_a,
    hidden_b,
    owner_pad,
    route,
    member,
    normed,
    state_sem,
    expand_sem,
    contract_sem,
):
    def chunk_of(c):
        return pl.ds(pl.multiple_of(c * CHUNK, CHUNK), CHUNK)

    def start(c):
        pltpu.make_async_copy(
            expand_hbm.at[:, chunk_of(c)], expand.at[c], expand_sem.at[c]
        ).start()
        pltpu.make_async_copy(
            contract_hbm.at[chunk_of(c), :], contract.at[c], contract_sem.at[c]
        ).start()

    def wait(c):
        pltpu.make_async_copy(
            expand_hbm.at[:, chunk_of(c)], expand.at[c], expand_sem.at[c]
        ).wait()
        pltpu.make_async_copy(
            contract_hbm.at[chunk_of(c), :], contract.at[c], contract_sem.at[c]
        ).wait()

    state_copy = pltpu.make_async_copy(states_hbm, states, state_sem)
    state_copy.start()
    for c in range(AHEAD):
        start(c)

    owner_pad[...] = jnp.full((8, NPAD), -4096, jnp.int32)
    owner_pad[0:1, 0:NODES] = owner_ref[...]
    owner = owner_pad[0:1, :]
    named = jnp.where(iota((PEERS, NPAD), 0) == owner, 1.0, 0.0).astype(bf16)
    before = jnp.where(iota((NPAD, NPAD), 0) < iota((NPAD, NPAD), 1), 1.0, 0.0).astype(bf16)
    earlier = dot(named, before)
    rank = jnp.sum(named.astype(f32) * earlier, axis=0, keepdims=True).astype(jnp.int32)
    own_row = owner * 8 + rank
    upper = upper_ref[0]
    beside = owner + jnp.where(upper == 1, 1, -1)
    edge = jnp.where(upper == 1, GROUP - 1, 0)
    has_beside = (owner & (GROUP - 1)) != edge
    halo_row = jnp.where(has_beside, beside * 8 + 2 + rank, -4096)
    target_ref[...] = jnp.where(iota((8, NPAD), 0) == 0, own_row, halo_row)
    rows = iota((ROWS, NPAD), 0)
    for u in range(2):
        shifted = rows - 4 * u
        hit = (shifted == own_row) | (shifted == halo_row)
        route[:, u * NPAD : (u + 1) * NPAD] = jnp.where(hit, 1.0, 0.0).astype(bf16)
    mask = jnp.where(iota((NPAD, TOKENS), 0) == node_ref[...], 1.0, 0.0)
    member[...] = mask.astype(bf16)
    counts = jnp.maximum(jnp.sum(mask, axis=1, keepdims=True), 1.0)

    def block_of(m):
        return pl.ds(m * BLOCK, BLOCK)

    def first(c, m):
        return dot(states[block_of(m), :], expand[c])

    def second(c, m, values):
        acted = 0.5 * values * (1.0 + lax.erf(values * ROOT_HALF))
        total[block_of(m), :] += dot(acted.astype(bf16), contract[c])

    state_copy.wait()
    total[...] = states[...].astype(f32)
    wait(0)
    hidden_a[...] = first(0, 0)
    buffers = (hidden_a, hidden_b)

    def step(c, carry):
        @pl.when(c + AHEAD < CHUNKS)
        def _():
            start(c + AHEAD)

        @pl.when(c + 1 < CHUNKS)
        def _():
            wait(c + 1)

        for m in range(BLOCKS):
            now, later = buffers[m % 2], buffers[(m + 1) % 2]
            if m + 1 < BLOCKS:
                later[...] = first(c, m + 1)
            else:
                later[...] = first(jnp.minimum(c + 1, CHUNKS - 1), 0)
            second(c, m, now[...])
        return carry

    lax.fori_loop(0, CHUNKS, step, 0)

    for m in range(BLOCKS):
        mixed = total[block_of(m), :]
        centred = mixed - jnp.mean(mixed, axis=1, keepdims=True)
        variance = jnp.mean(centred * centred, axis=1, keepdims=True)
        normed[block_of(m), :] = (centred * lax.rsqrt(variance + EPS)).astype(bf16)
    embeds = (dot(member[...], normed[...]) / counts).astype(bf16)
    stacked = jnp.concatenate([embeds[:, :HALF], embeds[:, HALF:]], axis=0)
    out_ref[...] = dot(route[...], stacked).astype(bf16)


def encode(upper, owner, node_ids, states, expand_weight, contract_weight):
    dma = pltpu.SemaphoreType.DMA
    return pl.pallas_call(
        encode_kernel,
        out_shape=(
            jax.ShapeDtypeStruct((ROWS, HALF), bf16),
            jax.ShapeDtypeStruct((8, NPAD), jnp.int32),
        ),
        in_specs=[SMEM, VMEM, VMEM, ANY, ANY, ANY],
        out_specs=(VMEM, VMEM),
        scratch_shapes=[
            pltpu.VMEM((TOKENS, D), bf16),
            pltpu.VMEM((CHUNKS, D, CHUNK), bf16),
            pltpu.VMEM((CHUNKS, CHUNK, D), bf16),
            pltpu.VMEM((TOKENS, D), f32),
            pltpu.VMEM((BLOCK, CHUNK), f32),
            pltpu.VMEM((BLOCK, CHUNK), f32),
            pltpu.VMEM((8, NPAD), jnp.int32),
            pltpu.VMEM((ROWS, 2 * NPAD), bf16),
            pltpu.VMEM((NPAD, TOKENS), bf16),
            pltpu.VMEM((TOKENS, D), bf16),
            dma,
            dma((CHUNKS,)),
            dma((CHUNKS,)),
        ],
        compiler_params=params(56),
        cost_estimate=cost(4 * TOKENS * D * FF, 20 * 2**20),
        name="encode",
    )(upper, owner, node_ids, states, expand_weight, contract_weight)


def prepare_kernel(
    columns_ref,
    count_ref,
    values_ref,
    target_ref,
    cotangent_ref,
    weight_ref,
    mix_ref,
    mix_t_ref,
    band_ref,
    pick_ref,
    inner_ref,
    low_ref,
    high_ref,
    band_t,
):
    band_ref[...] = jnp.zeros((SLOTS, 2 * SLOTS), bf16)
    band_t[...] = jnp.zeros((2 * SLOTS, SLOTS), bf16)
    for r in range(2):
        for c in range(r, r + 3):
            tile = jnp.zeros((TILE, TILE), f32)
            for s in range(3):
                used = (s < count_ref[0, r]) & (columns_ref[0, r, s] == c)
                tile += jnp.where(used, 1.0, 0.0) * values_ref[0, r, s].astype(f32)
            band_ref[r * TILE : (r + 1) * TILE, c * TILE : (c + 1) * TILE] = tile.astype(bf16)
            band_t[c * TILE : (c + 1) * TILE, r * TILE : (r + 1) * TILE] = tile.T.astype(bf16)

    def place(column, u):
        peer, slot = column >> 3, column & 3
        halo = jnp.where(peer < PEERS // 2, 2 * SLOTS - TILE, -PEERS) + 2 * peer + slot - 2
        source = jnp.where(slot < 2, TILE + 2 * peer + slot, halo)
        return jnp.where(((column >> 2) & 1) == u, source, -1)

    shape = (2 * SLOTS, ROWS)
    for u in range(2):
        moved = jnp.where(iota(shape, 0) == place(iota((1, ROWS), 1), u), 1.0, 0.0)
        mix_ref[u * SLOTS : (u + 1) * SLOTS, :] = dot(band_ref[...], moved.astype(bf16)).astype(bf16)
        back = jnp.where(iota(shape[::-1], 1) == place(iota((ROWS, 1), 0), u), 1.0, 0.0)
        mix_t_ref[:, u * SLOTS : (u + 1) * SLOTS] = dot(back.astype(bf16), band_t[...]).astype(bf16)

    diagonal = iota((NODES, NPAD), 0) == iota((NODES, NPAD), 1)
    own_row = jnp.sum(jnp.where(diagonal, target_ref[0:1, :], 0), axis=1, keepdims=True)
    halo_row = jnp.sum(jnp.where(diagonal, target_ref[1:2, :], 0), axis=1, keepdims=True)
    lanes = iota((NODES, ROWS), 1)
    for u in range(2):
        hit = (lanes - 4 * u == own_row) | (lanes - 4 * u == halo_row)
        pick_ref[u * NODES : (u + 1) * NODES, :] = jnp.where(hit, 1.0, 0.0).astype(bf16)

    grad_mix = dot_t(cotangent_ref[...], weight_ref[...]).astype(bf16)
    spread = dot(band_t[...], grad_mix)
    low_ref[...] = spread[:TILE].astype(bf16)
    inner_ref[...] = spread[TILE : TILE + SLOTS]
    high_ref[...] = spread[TILE + SLOTS :].astype(bf16)


def prepare(columns, counts, values, target, cotangent, weight):
    return pl.pallas_call(
        prepare_kernel,
        out_shape=(
            jax.ShapeDtypeStruct((2 * SLOTS, ROWS), bf16),
            jax.ShapeDtypeStruct((ROWS, 2 * SLOTS), bf16),
            jax.ShapeDtypeStruct((SLOTS, 2 * SLOTS), bf16),
            jax.ShapeDtypeStruct((2 * NODES, ROWS), bf16),
            jax.ShapeDtypeStruct((SLOTS, D), f32),
            jax.ShapeDtypeStruct((TILE, D), bf16),
            jax.ShapeDtypeStruct((TILE, D), bf16),
        ),
        in_specs=[SMEM, SMEM, VMEM, VMEM, VMEM, VMEM],
        out_specs=(VMEM,) * 7,
        scratch_shapes=[pltpu.VMEM((2 * SLOTS, SLOTS), bf16)],
        compiler_params=params(40),
        cost_estimate=cost(2 * 10**9, 10 * 2**20),
        name="prepare",
    )(columns, counts, values, target, cotangent, weight)


def middle_kernel(
    rows_hbm,
    mix_hbm,
    weight_hbm,
    inner_hbm,
    left_hbm,
    right_hbm,
    mix_t_hbm,
    top_ref,
    bottom_ref,
    out_ref,
    rows,
    mix,
    weight,
    inner,
    left,
    right,
    mix_t,
    sems,
):
    pairs = (
        (mix_hbm, mix),
        (rows_hbm, rows),
        (weight_hbm, weight),
        (inner_hbm, inner),
        (left_hbm, left),
        (right_hbm, right),
        (mix_t_hbm, mix_t),
    )
    copies = [pltpu.make_async_copy(a, b, sems.at[i]) for i, (a, b) in enumerate(pairs)]
    for copy in copies:
        copy.start()
    copies[0].wait()
    copies[1].wait()
    halves = dot(mix[...], rows[...]).astype(bf16)
    mixed = jnp.concatenate([halves[:SLOTS], halves[SLOTS:]], axis=1)
    copies[2].wait()
    before = dot(mixed, weight[...])
    erf = 0.5 * (1.0 + lax.erf(before * ROOT_HALF))
    acted = (before * erf).astype(bf16)
    top_ref[...] = acted[:TILE]
    bottom_ref[...] = acted[TILE:]
    slope = erf + before * (INV_ROOT_TAU * jnp.exp(-0.5 * before * before))
    for copy in copies[3:6]:
        copy.wait()
    rims = jnp.concatenate([left[...], right[...]], axis=0).astype(f32)
    grad_before = ((inner[...] + rims) * slope).astype(bf16)
    grad_mix = dot_t(grad_before, weight[...]).astype(bf16)
    stacked = jnp.concatenate([grad_mix[:, :HALF], grad_mix[:, HALF:]], axis=0)
    copies[6].wait()
    out_ref[...] = dot(mix_t[...], stacked).astype(bf16)


def middle(*arrays):
    return pl.pallas_call(
        middle_kernel,
        out_shape=(
            jax.ShapeDtypeStruct((TILE, D), bf16),
            jax.ShapeDtypeStruct((TILE, D), bf16),
            jax.ShapeDtypeStruct((ROWS, HALF), bf16),
        ),
        in_specs=[ANY] * 7,
        out_specs=(VMEM,) * 3,
        scratch_shapes=[pltpu.VMEM(a.shape, a.dtype) for a in arrays]
        + [pltpu.SemaphoreType.DMA((7,))],
        compiler_params=params(24),
        cost_estimate=cost(3 * 10**9, 8 * 2**20),
        name="middle",
    )(*arrays)


def finish_kernel(left_hbm, top_hbm, bottom_hbm, right_hbm, band_hbm, weight_hbm, out_ref, wide, band, weight, sems):
    sources = (left_hbm, top_hbm, bottom_hbm, right_hbm)
    copies = [
        pltpu.make_async_copy(a, wide.at[pl.ds(i * TILE, TILE), :], sems.at[i])
        for i, a in enumerate(sources)
    ]
    copies.append(pltpu.make_async_copy(band_hbm, band, sems.at[4]))
    copies.append(pltpu.make_async_copy(weight_hbm, weight, sems.at[5]))
    for copy in copies:
        copy.start()
    for copy in copies[:5]:
        copy.wait()
    mixed = dot(band[...], wide[...]).astype(bf16)
    copies[5].wait()
    out_ref[...] = dot(mixed, weight[...]).astype(bf16)


def finish(*arrays):
    return pl.pallas_call(
        finish_kernel,
        out_shape=jax.ShapeDtypeStruct((SLOTS, D), bf16),
        in_specs=[ANY] * 6,
        out_specs=VMEM,
        scratch_shapes=[
            pltpu.VMEM((2 * SLOTS, D), bf16),
            pltpu.VMEM((SLOTS, 2 * SLOTS), bf16),
            pltpu.VMEM((D, D), bf16),
            pltpu.SemaphoreType.DMA((6,)),
        ],
        compiler_params=params(16),
        cost_estimate=cost(10**9, 5 * 2**20),
        name="finish",
    )(*arrays)


def gather_kernel(pick_ref, rows_ref, out_ref):
    for u in range(2):
        picked = dot(pick_ref[u * NODES : (u + 1) * NODES, :], rows_ref[...])
        out_ref[:, u * HALF : (u + 1) * HALF] = picked.astype(bf16)


def gather(pick, rows):
    return pl.pallas_call(
        gather_kernel,
        out_shape=jax.ShapeDtypeStruct((NODES, D), bf16),
        in_specs=[VMEM, VMEM],
        out_specs=VMEM,
        compiler_params=params(16),
        cost_estimate=cost(4 * 10**8, 2 * 2**20),
        name="gather",
    )(pick, rows)


def swap(rows):
    return lax.all_to_all(
        rows.reshape(PEERS, 8, HALF), ("enc", "dom"), split_axis=0, concat_axis=0, tiled=True
    ).reshape(ROWS, HALF)


def local(
    token_states,
    token_nodes,
    expand_weight,
    contract_weight,
    node_owner,
    tile_columns,
    tile_count,
    tile_values,
    first_weight,
    second_weight,
    output_cotangent,
):
    device = lax.axis_index("enc") * GROUP + lax.axis_index("dom")
    upper = (device >= PEERS // 2).astype(jnp.int32).reshape(1)
    rightward = [(i, i + 1) for i in range(GROUP - 1)]
    leftward = [(i + 1, i) for i in range(GROUP - 1)]
    outgoing, target = encode(
        upper, node_owner.reshape(1, NODES), token_nodes, token_states, expand_weight, contract_weight
    )
    arrived = swap(outgoing)
    mix, mix_t, band, pick, inner, low, high = prepare(
        tile_columns, tile_count, tile_values, target, output_cotangent, second_weight
    )
    from_right = lax.ppermute(low, "dom", leftward)
    from_left = lax.ppermute(high, "dom", rightward)
    top, bottom, grads = middle(arrived, mix, first_weight, inner, from_left, from_right, mix_t)
    returned = swap(grads)
    left = lax.ppermute(bottom, "dom", rightward)
    right = lax.ppermute(top, "dom", leftward)
    graph_output = finish(left, top, bottom, right, band, second_weight)
    return (graph_output, gather(pick, returned))


def solution(mesh):
    rows = ("enc", "dom")
    placed = (
        P(rows, None),
        P(rows, None),
        P(),
        P(),
        P(rows, None),
        P(rows, None, None),
        P(rows, None),
        P(rows, None, None, None, None),
        P(),
        P(),
        P(rows, None),
    )
    return jax.shard_map(
        local,
        mesh=mesh,
        in_specs=placed,
        out_specs=(P(rows, None), P(rows, None)),
        check_vma=False,
    )
```

```python
import jax
import jax.numpy as jnp
from jax import lax
from jax.experimental import pallas as pl
from jax.experimental.pallas import tpu as pltpu
from jax.sharding import PartitionSpec as P

NODES = 192
NPAD = 256
TOKENS = 1024
D = 1024
FF = 4096
HALF = 512
PEERS = 128
GROUP = 8
ROWS = 1024
TILE = 128
SLOTS = 256

CHUNK = 512
CHUNKS = FF // CHUNK
BLOCK = 256
BLOCKS = TOKENS // BLOCK
AHEAD = 2
PIECES = 4

bf16 = jnp.bfloat16
f32 = jnp.float32
EPS = 1e-07
ROOT_HALF = 0.7071067811865476
INV_ROOT_TAU = 0.3989422804014327

ANY = pl.BlockSpec(memory_space=pl.ANY)
VMEM = pl.BlockSpec(memory_space=pltpu.VMEM)
SMEM = pl.BlockSpec(memory_space=pltpu.SMEM)


def dot(a, b):
    return jnp.dot(a, b, preferred_element_type=f32)


def dot_t(a, b):
    return lax.dot_general(a, b, (((1,), (1,)), ((), ())), preferred_element_type=f32)


def iota(shape, dim):
    return lax.broadcasted_iota(jnp.int32, shape, dim)


def params(mib):
    return pltpu.CompilerParams(vmem_limit_bytes=mib * 2**20)


def cost(flops, moved):
    return pl.CostEstimate(flops=flops, bytes_accessed=moved, transcendentals=0)


def send_rows(rows_of, out, out_hbm, sem):
    size = ROWS // PIECES
    copies = []
    for i in range(PIECES):
        rows = pl.ds(i * size, size)
        out[rows, :] = rows_of(rows).astype(bf16)
        copies.append(pltpu.make_async_copy(out.at[rows, :], out_hbm.at[rows, :], sem.at[i]))
        copies[-1].start()
    for copy in copies:
        copy.wait()


def encode_kernel(
    upper_ref,
    owner_ref,
    node_ref,
    states_hbm,
    expand_hbm,
    contract_hbm,
    out_hbm,
    target_ref,
    out,
    states,
    expand,
    contract,
    total,
    hidden_a,
    hidden_b,
    owner_pad,
    route,
    member,
    normed,
    state_sem,
    expand_sem,
    contract_sem,
    out_sem,
):
    def block_of(m):
        return pl.ds(m * BLOCK, BLOCK)

    def chunk_of(c):
        return pl.ds(pl.multiple_of(c * CHUNK, CHUNK), CHUNK)

    def start(c):
        pltpu.make_async_copy(
            expand_hbm.at[:, chunk_of(c)], expand.at[c], expand_sem.at[c]
        ).start()
        pltpu.make_async_copy(
            contract_hbm.at[chunk_of(c), :], contract.at[c], contract_sem.at[c]
        ).start()

    def wait(c):
        pltpu.make_async_copy(
            expand_hbm.at[:, chunk_of(c)], expand.at[c], expand_sem.at[c]
        ).wait()
        pltpu.make_async_copy(
            contract_hbm.at[chunk_of(c), :], contract.at[c], contract_sem.at[c]
        ).wait()

    def state_copy(m):
        return pltpu.make_async_copy(
            states_hbm.at[block_of(m), :], states.at[block_of(m), :], state_sem.at[m]
        )

    state_copy(0).start()
    start(0)
    for m in range(1, BLOCKS):
        state_copy(m).start()
    for c in range(1, AHEAD):
        start(c)

    owner_pad[...] = jnp.full((8, NPAD), -4096, jnp.int32)
    owner_pad[0:1, 0:NODES] = owner_ref[...]
    owner = owner_pad[0:1, :]
    named = jnp.where(iota((PEERS, NPAD), 0) == owner, 1.0, 0.0).astype(bf16)
    before = jnp.where(iota((NPAD, NPAD), 0) < iota((NPAD, NPAD), 1), 1.0, 0.0).astype(bf16)
    earlier = dot(named, before)
    rank = jnp.sum(named.astype(f32) * earlier, axis=0, keepdims=True).astype(jnp.int32)
    own_row = owner * 8 + rank
    upper = upper_ref[0]
    beside = owner + jnp.where(upper == 1, 1, -1)
    edge = jnp.where(upper == 1, GROUP - 1, 0)
    has_beside = (owner & (GROUP - 1)) != edge
    halo_row = jnp.where(has_beside, beside * 8 + 2 + rank, -4096)
    target_ref[...] = jnp.where(iota((8, NPAD), 0) == 0, own_row, halo_row)
    rows = iota((ROWS, NPAD), 0)
    for u in range(2):
        shifted = rows - 4 * u
        hit = (shifted == own_row) | (shifted == halo_row)
        route[:, u * NPAD : (u + 1) * NPAD] = jnp.where(hit, 1.0, 0.0).astype(bf16)
    mask = jnp.where(iota((NPAD, TOKENS), 0) == node_ref[...], 1.0, 0.0)
    member[...] = mask.astype(bf16)
    counts = jnp.maximum(jnp.sum(mask, axis=1, keepdims=True), 1.0)

    def first(c, m):
        return dot(states[block_of(m), :], expand[c])

    def second(c, m, values):
        acted = 0.5 * values * (1.0 + lax.erf(values * ROOT_HALF))
        total[block_of(m), :] += dot(acted.astype(bf16), contract[c])

    buffers = (hidden_a, hidden_b)
    for m in range(BLOCKS):
        state_copy(m).wait()
        total[block_of(m), :] = states[block_of(m), :].astype(f32)
        if m == 0:
            wait(0)
            hidden_a[...] = first(0, 0)

    def step(c, carry):
        @pl.when(c + AHEAD < CHUNKS)
        def _():
            start(c + AHEAD)

        wait(c + 1)
        for m in range(BLOCKS):
            now, later = buffers[m % 2], buffers[(m + 1) % 2]
            if m + 1 < BLOCKS:
                later[...] = first(c, m + 1)
            else:
                later[...] = first(c + 1, 0)
            second(c, m, now[...])
        return carry

    lax.fori_loop(0, CHUNKS - 1, step, 0)

    for m in range(BLOCKS):
        now, later = buffers[m % 2], buffers[(m + 1) % 2]
        if m + 1 < BLOCKS:
            later[...] = first(CHUNKS - 1, m + 1)
        second(CHUNKS - 1, m, now[...])
        mixed = total[block_of(m), :]
        centred = mixed - jnp.mean(mixed, axis=1, keepdims=True)
        variance = jnp.mean(centred * centred, axis=1, keepdims=True)
        normed[block_of(m), :] = (centred * lax.rsqrt(variance + EPS)).astype(bf16)
    summed = dot(member[...], normed[...])
    embeds = (summed / counts).astype(bf16)
    stacked = jnp.concatenate([embeds[:, :HALF], embeds[:, HALF:]], axis=0)
    send_rows(lambda r: dot(route[r, :], stacked), out, out_hbm, out_sem)


def encode(upper, owner, node_ids, states, expand_weight, contract_weight):
    dma = pltpu.SemaphoreType.DMA
    return pl.pallas_call(
        encode_kernel,
        out_shape=(
            jax.ShapeDtypeStruct((ROWS, HALF), bf16),
            jax.ShapeDtypeStruct((8, NPAD), jnp.int32),
        ),
        in_specs=[SMEM, VMEM, VMEM, ANY, ANY, ANY],
        out_specs=(ANY, VMEM),
        scratch_shapes=[
            pltpu.VMEM((ROWS, HALF), bf16),
            pltpu.VMEM((TOKENS, D), bf16),
            pltpu.VMEM((CHUNKS, D, CHUNK), bf16),
            pltpu.VMEM((CHUNKS, CHUNK, D), bf16),
            pltpu.VMEM((TOKENS, D), f32),
            pltpu.VMEM((BLOCK, CHUNK), f32),
            pltpu.VMEM((BLOCK, CHUNK), f32),
            pltpu.VMEM((8, NPAD), jnp.int32),
            pltpu.VMEM((ROWS, 2 * NPAD), bf16),
            pltpu.VMEM((NPAD, TOKENS), bf16),
            pltpu.VMEM((TOKENS, D), bf16),
            dma((BLOCKS,)),
            dma((CHUNKS,)),
            dma((CHUNKS,)),
            dma((PIECES,)),
        ],
        compiler_params=params(56),
        cost_estimate=cost(4 * TOKENS * D * FF, 20 * 2**20),
        name="encode",
    )(upper, owner, node_ids, states, expand_weight, contract_weight)


def prepare_kernel(
    columns_ref,
    count_ref,
    values_ref,
    cotangent_ref,
    weight_ref,
    mix_ref,
    mix_t_ref,
    band_ref,
    inner_ref,
    low_ref,
    high_ref,
    band_t,
):
    band_ref[...] = jnp.zeros((SLOTS, 2 * SLOTS), bf16)
    band_t[...] = jnp.zeros((2 * SLOTS, SLOTS), bf16)
    for r in range(2):
        for c in range(r, r + 3):
            tile = jnp.zeros((TILE, TILE), f32)
            for s in range(3):
                used = (s < count_ref[0, r]) & (columns_ref[0, r, s] == c)
                tile += jnp.where(used, 1.0, 0.0) * values_ref[0, r, s].astype(f32)
            band_ref[r * TILE : (r + 1) * TILE, c * TILE : (c + 1) * TILE] = tile.astype(bf16)
            band_t[c * TILE : (c + 1) * TILE, r * TILE : (r + 1) * TILE] = tile.T.astype(bf16)

    def place(column, u):
        peer, slot = column >> 3, column & 3
        halo = jnp.where(peer < PEERS // 2, 2 * SLOTS - TILE, -PEERS) + 2 * peer + slot - 2
        source = jnp.where(slot < 2, TILE + 2 * peer + slot, halo)
        return jnp.where(((column >> 2) & 1) == u, source, -1)

    shape = (2 * SLOTS, ROWS)
    for u in range(2):
        moved = jnp.where(iota(shape, 0) == place(iota((1, ROWS), 1), u), 1.0, 0.0)
        mix_ref[u * SLOTS : (u + 1) * SLOTS, :] = dot(band_ref[...], moved.astype(bf16)).astype(bf16)
        back = jnp.where(iota(shape[::-1], 1) == place(iota((ROWS, 1), 0), u), 1.0, 0.0)
        mix_t_ref[:, u * SLOTS : (u + 1) * SLOTS] = dot(back.astype(bf16), band_t[...]).astype(bf16)

    grad_mix = dot_t(cotangent_ref[...], weight_ref[...]).astype(bf16)
    spread = dot(band_t[...], grad_mix)
    low_ref[...] = spread[:TILE].astype(bf16)
    inner_ref[...] = spread[TILE : TILE + SLOTS]
    high_ref[...] = spread[TILE + SLOTS :].astype(bf16)


def prepare(columns, counts, values, cotangent, weight):
    return pl.pallas_call(
        prepare_kernel,
        out_shape=(
            jax.ShapeDtypeStruct((2 * SLOTS, ROWS), bf16),
            jax.ShapeDtypeStruct((ROWS, 2 * SLOTS), bf16),
            jax.ShapeDtypeStruct((SLOTS, 2 * SLOTS), bf16),
            jax.ShapeDtypeStruct((SLOTS, D), f32),
            jax.ShapeDtypeStruct((TILE, D), bf16),
            jax.ShapeDtypeStruct((TILE, D), bf16),
        ),
        in_specs=[SMEM, SMEM, VMEM, VMEM, VMEM],
        out_specs=(VMEM,) * 6,
        scratch_shapes=[pltpu.VMEM((2 * SLOTS, SLOTS), bf16)],
        compiler_params=params(40),
        cost_estimate=cost(2 * 10**9, 10 * 2**20),
        name="prepare",
    )(columns, counts, values, cotangent, weight)


def middle_kernel(
    rows_hbm,
    mix_hbm,
    weight_hbm,
    inner_hbm,
    left_hbm,
    right_hbm,
    mix_t_hbm,
    top_hbm,
    bottom_hbm,
    out_hbm,
    acts,
    out,
    rows,
    mix,
    weight,
    inner,
    left,
    right,
    mix_t,
    sems,
    act_sems,
    out_sems,
):
    pairs = (
        (mix_hbm, mix),
        (rows_hbm, rows),
        (weight_hbm, weight),
        (inner_hbm, inner),
        (left_hbm, left),
        (right_hbm, right),
        (mix_t_hbm, mix_t),
    )
    copies = [pltpu.make_async_copy(a, b, sems.at[i]) for i, (a, b) in enumerate(pairs)]
    for copy in copies:
        copy.start()
    copies[0].wait()
    copies[1].wait()
    halves = dot(mix[...], rows[...]).astype(bf16)
    mixed = jnp.concatenate([halves[:SLOTS], halves[SLOTS:]], axis=1)
    copies[2].wait()
    before = dot(mixed, weight[...])
    erf = 0.5 * (1.0 + lax.erf(before * ROOT_HALF))
    acted = (before * erf).astype(bf16)
    acts[...] = acted
    act_copies = [
        pltpu.make_async_copy(acts.at[pl.ds(i * TILE, TILE), :], to, act_sems.at[i])
        for i, to in enumerate((top_hbm, bottom_hbm))
    ]
    for copy in act_copies:
        copy.start()
    slope = erf + before * (INV_ROOT_TAU * jnp.exp(-0.5 * before * before))
    for copy in copies[3:6]:
        copy.wait()
    rims = jnp.concatenate([left[...], right[...]], axis=0).astype(f32)
    grad_before = ((inner[...] + rims) * slope).astype(bf16)
    grad_mix = dot_t(grad_before, weight[...]).astype(bf16)
    stacked = jnp.concatenate([grad_mix[:, :HALF], grad_mix[:, HALF:]], axis=0)
    copies[6].wait()
    send_rows(lambda r: dot(mix_t[r, :], stacked), out, out_hbm, out_sems)
    for copy in act_copies:
        copy.wait()


def middle(*arrays):
    return pl.pallas_call(
        middle_kernel,
        out_shape=(
            jax.ShapeDtypeStruct((TILE, D), bf16),
            jax.ShapeDtypeStruct((TILE, D), bf16),
            jax.ShapeDtypeStruct((ROWS, HALF), bf16),
        ),
        in_specs=[ANY] * 7,
        out_specs=(ANY,) * 3,
        scratch_shapes=[pltpu.VMEM((SLOTS, D), bf16), pltpu.VMEM((ROWS, HALF), bf16)]
        + [pltpu.VMEM(a.shape, a.dtype) for a in arrays]
        + [pltpu.SemaphoreType.DMA((n,)) for n in (7, 2, PIECES)],
        compiler_params=params(62),
        cost_estimate=cost(3 * 10**9, 8 * 2**20),
        name="middle",
    )(*arrays)


def finish_kernel(left_hbm, top_hbm, bottom_hbm, right_hbm, band_hbm, weight_hbm, out_ref, wide, band, weight, sems):
    sources = (left_hbm, top_hbm, bottom_hbm, right_hbm)
    copies = [
        pltpu.make_async_copy(a, wide.at[pl.ds(i * TILE, TILE), :], sems.at[i])
        for i, a in enumerate(sources)
    ]
    copies.append(pltpu.make_async_copy(band_hbm, band, sems.at[4]))
    copies.append(pltpu.make_async_copy(weight_hbm, weight, sems.at[5]))
    for copy in copies:
        copy.start()
    for copy in copies[:5]:
        copy.wait()
    mixed = dot(band[...], wide[...]).astype(bf16)
    copies[5].wait()
    out_ref[...] = dot(mixed, weight[...]).astype(bf16)


def finish(*arrays):
    return pl.pallas_call(
        finish_kernel,
        out_shape=jax.ShapeDtypeStruct((SLOTS, D), bf16),
        in_specs=[ANY] * 6,
        out_specs=VMEM,
        scratch_shapes=[
            pltpu.VMEM((2 * SLOTS, D), bf16),
            pltpu.VMEM((SLOTS, 2 * SLOTS), bf16),
            pltpu.VMEM((D, D), bf16),
            pltpu.SemaphoreType.DMA((6,)),
        ],
        compiler_params=params(16),
        cost_estimate=cost(10**9, 5 * 2**20),
        name="finish",
    )(*arrays)


def gather_kernel(target_ref, rows_ref, out_ref, pick):
    diagonal = iota((NODES, NPAD), 0) == iota((NODES, NPAD), 1)
    own_row = jnp.sum(jnp.where(diagonal, target_ref[0:1, :], 0), axis=1, keepdims=True)
    halo_row = jnp.sum(jnp.where(diagonal, target_ref[1:2, :], 0), axis=1, keepdims=True)
    lanes = iota((NODES, ROWS), 1)
    for u in range(2):
        hit = (lanes - 4 * u == own_row) | (lanes - 4 * u == halo_row)
        pick[u * NODES : (u + 1) * NODES, :] = jnp.where(hit, 1.0, 0.0).astype(bf16)
    for u in range(2):
        picked = dot(pick[u * NODES : (u + 1) * NODES, :], rows_ref[...])
        out_ref[:, u * HALF : (u + 1) * HALF] = picked.astype(bf16)


def gather(target, rows):
    return pl.pallas_call(
        gather_kernel,
        out_shape=jax.ShapeDtypeStruct((NODES, D), bf16),
        in_specs=[VMEM, VMEM],
        out_specs=VMEM,
        scratch_shapes=[pltpu.VMEM((2 * NODES, ROWS), bf16)],
        compiler_params=params(16),
        cost_estimate=cost(4 * 10**8, 2 * 2**20),
        name="gather",
    )(target, rows)


def swap(rows):
    return lax.all_to_all(
        rows.reshape(PEERS, 8, HALF), ("enc", "dom"), split_axis=0, concat_axis=0, tiled=True
    ).reshape(ROWS, HALF)


def local(
    token_states,
    token_nodes,
    expand_weight,
    contract_weight,
    node_owner,
    tile_columns,
    tile_count,
    tile_values,
    first_weight,
    second_weight,
    output_cotangent,
):
    device = lax.axis_index("enc") * GROUP + lax.axis_index("dom")
    upper = (device >= PEERS // 2).astype(jnp.int32).reshape(1)
    rightward = [(i, i + 1) for i in range(GROUP - 1)]
    leftward = [(i + 1, i) for i in range(GROUP - 1)]
    outgoing, target = encode(
        upper, node_owner.reshape(1, NODES), token_nodes, token_states, expand_weight, contract_weight
    )
    arrived = swap(outgoing)
    target, later_cotangent = lax.optimization_barrier((target, output_cotangent))
    mix, mix_t, band, inner, low, high = prepare(
        tile_columns, tile_count, tile_values, later_cotangent, second_weight
    )
    from_right = lax.ppermute(low, "dom", leftward)
    from_left = lax.ppermute(high, "dom", rightward)
    top, bottom, grads = middle(arrived, mix, first_weight, inner, from_left, from_right, mix_t)
    returned = swap(grads)
    left = lax.ppermute(bottom, "dom", rightward)
    right = lax.ppermute(top, "dom", leftward)
    graph_output = finish(left, top, bottom, right, band, second_weight)
    return (graph_output, gather(target, returned))


def solution(mesh):
    rows = ("enc", "dom")
    placed = (
        P(rows, None),
        P(rows, None),
        P(),
        P(),
        P(rows, None),
        P(rows, None, None),
        P(rows, None),
        P(rows, None, None, None, None),
        P(),
        P(),
        P(rows, None),
    )
    return jax.shard_map(
        local,
        mesh=mesh,
        in_specs=placed,
        out_specs=(P(rows, None), P(rows, None)),
        check_vma=False,
    )
```

```python
import jax
import jax.numpy as jnp
from jax import lax
from jax.experimental import pallas as pl
from jax.experimental.pallas import tpu as pltpu
from jax.sharding import PartitionSpec as P

NODES = 192
NPAD = 256
TOKENS = 1024
D = 1024
FF = 4096
HALF = 512
PEERS = 128
GROUP = 8
ROWS = 1024
TILE = 128
SLOTS = 256

CHUNK = 512
CHUNKS = FF // CHUNK
BLOCK = 512
BLOCKS = TOKENS // BLOCK
AHEAD = 2
PIECES = 4

bf16 = jnp.bfloat16
f32 = jnp.float32
EPS = 1e-07
ROOT_HALF = 0.7071067811865476
INV_ROOT_TAU = 0.3989422804014327

ANY = pl.BlockSpec(memory_space=pl.ANY)
VMEM = pl.BlockSpec(memory_space=pltpu.VMEM)
SMEM = pl.BlockSpec(memory_space=pltpu.SMEM)


def dot(a, b):
    return jnp.dot(a, b, preferred_element_type=f32)


def dot_t(a, b):
    return lax.dot_general(a, b, (((1,), (1,)), ((), ())), preferred_element_type=f32)


def iota(shape, dim):
    return lax.broadcasted_iota(jnp.int32, shape, dim)


def params(mib):
    return pltpu.CompilerParams(vmem_limit_bytes=int(mib * 2**20))


def cost(flops, moved):
    return pl.CostEstimate(flops=flops, bytes_accessed=moved, transcendentals=0)


def send_rows(rows_of, out, out_hbm, sem):
    size = ROWS // PIECES
    copies = []
    for i in range(PIECES):
        rows = pl.ds(i * size, size)
        out[rows, :] = rows_of(rows).astype(bf16)
        copies.append(pltpu.make_async_copy(out.at[rows, :], out_hbm.at[rows, :], sem.at[i]))
        copies[-1].start()
    for copy in copies:
        copy.wait()


def encode_kernel(
    upper_ref,
    owner_ref,
    node_ref,
    states_hbm,
    expand_hbm,
    contract_hbm,
    out_hbm,
    target_ref,
    out,
    states,
    expand,
    contract,
    total,
    hidden_a,
    hidden_b,
    owner_pad,
    route,
    member,
    normed,
    state_sem,
    expand_sem,
    contract_sem,
    out_sem,
):
    def block_of(m):
        return pl.ds(m * BLOCK, BLOCK)

    def chunk_of(c):
        return pl.ds(pl.multiple_of(c * CHUNK, CHUNK), CHUNK)

    def start_expand(c):
        pltpu.make_async_copy(
            expand_hbm.at[:, chunk_of(c)], expand.at[c], expand_sem.at[c]
        ).start()

    def start(c):
        if not isinstance(c, int) or c > 0:
            start_expand(c)
        pltpu.make_async_copy(
            contract_hbm.at[chunk_of(c), :], contract.at[c], contract_sem.at[c]
        ).start()

    def wait_expand(c):
        pltpu.make_async_copy(
            expand_hbm.at[:, chunk_of(c)], expand.at[c], expand_sem.at[c]
        ).wait()

    def wait(c):
        if not isinstance(c, int) or c > 0:
            wait_expand(c)
        pltpu.make_async_copy(
            contract_hbm.at[chunk_of(c), :], contract.at[c], contract_sem.at[c]
        ).wait()

    def state_copy(m):
        return pltpu.make_async_copy(
            states_hbm.at[block_of(m), :], states.at[block_of(m), :], state_sem.at[m]
        )

    state_copy(0).start()
    start_expand(0)
    for m in range(1, BLOCKS):
        state_copy(m).start()
    start(0)

    owner_pad[...] = jnp.full((8, NPAD), -4096, jnp.int32)
    owner_pad[0:1, 0:NODES] = owner_ref[...]
    owner = owner_pad[0:1, :]
    named = jnp.where(iota((PEERS, NPAD), 0) == owner, 1.0, 0.0).astype(bf16)
    before = jnp.where(iota((NPAD, NPAD), 0) < iota((NPAD, NPAD), 1), 1.0, 0.0).astype(bf16)
    earlier = dot(named, before)
    rank = jnp.sum(named.astype(f32) * earlier, axis=0, keepdims=True).astype(jnp.int32)
    own_row = owner * 8 + rank
    upper = upper_ref[0]
    beside = owner + jnp.where(upper == 1, 1, -1)
    edge = jnp.where(upper == 1, GROUP - 1, 0)
    has_beside = (owner & (GROUP - 1)) != edge
    halo_row = jnp.where(has_beside, beside * 8 + 2 + rank, -4096)
    target_ref[...] = jnp.where(iota((8, NPAD), 0) == 0, own_row, halo_row)
    rows = iota((ROWS, NPAD), 0)
    for u in range(2):
        shifted = rows - 4 * u
        hit = (shifted == own_row) | (shifted == halo_row)
        route[:, u * NPAD : (u + 1) * NPAD] = jnp.where(hit, 1.0, 0.0).astype(bf16)
    mask = jnp.where(iota((NPAD, TOKENS), 0) == node_ref[...], 1.0, 0.0)
    member[...] = mask.astype(bf16)
    counts = jnp.maximum(jnp.sum(mask, axis=1, keepdims=True), 1.0)


    def first(c, m):
        return dot(states[block_of(m), :], expand[c])

    def second(c, m, values, opening):
        acted = 0.5 * values * (1.0 + lax.erf(values * ROOT_HALF))
        product = dot(acted.astype(bf16), contract[c])
        total[block_of(m), :] = product if opening else total[block_of(m), :] + product

    buffers = (hidden_a, hidden_b)

    def step(c, opening=False, closing=False):
        for m in range(BLOCKS):
            now, later = buffers[m % 2], buffers[(m + 1) % 2]
            if m + 1 < BLOCKS:
                later[...] = first(c, m + 1)
            elif not closing:
                if opening:
                    start(2)
                    wait(1)
                later[...] = first(c + 1, 0)
            second(c, m, now[...], opening)
            if closing:
                settle(m)

    def settle(m):
        mixed = total[block_of(m), :] + states[block_of(m), :].astype(f32)
        centred = mixed - jnp.mean(mixed, axis=1, keepdims=True)
        variance = jnp.mean(centred * centred, axis=1, keepdims=True)
        normed[block_of(m), :] = (centred * lax.rsqrt(variance + EPS)).astype(bf16)

    state_copy(0).wait()
    wait_expand(0)
    start(1)
    hidden_a[...] = first(0, 0)
    for m in range(1, BLOCKS):
        state_copy(m).wait()
    wait(0)
    step(0, opening=True)

    def middle_step(c, carry):
        @pl.when(c + AHEAD < CHUNKS)
        def _():
            start(c + AHEAD)

        wait(c + 1)
        step(c)
        return carry

    lax.fori_loop(1, CHUNKS - 1, middle_step, 0)
    step(CHUNKS - 1, closing=True)
    summed = dot(member[...], normed[...])
    embeds = (summed / counts).astype(bf16)
    stacked = jnp.concatenate([embeds[:, :HALF], embeds[:, HALF:]], axis=0)
    send_rows(lambda r: dot(route[r, :], stacked), out, out_hbm, out_sem)


def encode(upper, owner, node_ids, states, expand_weight, contract_weight):
    dma = pltpu.SemaphoreType.DMA
    return pl.pallas_call(
        encode_kernel,
        out_shape=(
            jax.ShapeDtypeStruct((ROWS, HALF), bf16),
            jax.ShapeDtypeStruct((8, NPAD), jnp.int32),
        ),
        in_specs=[SMEM, VMEM, VMEM, ANY, ANY, ANY],
        out_specs=(ANY, VMEM),
        scratch_shapes=[
            pltpu.VMEM((ROWS, HALF), bf16),
            pltpu.VMEM((TOKENS, D), bf16),
            pltpu.VMEM((CHUNKS, D, CHUNK), bf16),
            pltpu.VMEM((CHUNKS, CHUNK, D), bf16),
            pltpu.VMEM((TOKENS, D), f32),
            pltpu.VMEM((BLOCK, CHUNK), f32),
            pltpu.VMEM((BLOCK, CHUNK), f32),
            pltpu.VMEM((8, NPAD), jnp.int32),
            pltpu.VMEM((ROWS, 2 * NPAD), bf16),
            pltpu.VMEM((NPAD, TOKENS), bf16),
            pltpu.VMEM((TOKENS, D), bf16),
            dma((BLOCKS,)),
            dma((CHUNKS,)),
            dma((CHUNKS,)),
            dma((PIECES,)),
        ],
        compiler_params=params(56),
        cost_estimate=cost(4 * TOKENS * D * FF, 20 * 2**20),
        name="encode",
    )(upper, owner, node_ids, states, expand_weight, contract_weight)


def fill_band(columns_ref, count_ref, values_ref, band, transposed):
    band[...] = jnp.zeros(band.shape, bf16)
    for r in range(2):
        for c in range(r, r + 3):
            tile = jnp.zeros((TILE, TILE), f32)
            for s in range(3):
                used = (s < count_ref[0, r]) & (columns_ref[0, r, s] == c)
                tile += jnp.where(used, 1.0, 0.0) * values_ref[0, r, s].astype(f32)
            rows, lanes = slice(r * TILE, (r + 1) * TILE), slice(c * TILE, (c + 1) * TILE)
            if transposed:
                band[lanes, rows] = tile.T.astype(bf16)
            else:
                band[rows, lanes] = tile.astype(bf16)


def spread_kernel(
    columns_ref, count_ref, values_ref, cotangent_ref, weight_ref, low_ref, high_ref, inner_hbm, band_t, inner, sem
):
    fill_band(columns_ref, count_ref, values_ref, band_t, True)
    grad_mix = dot_t(cotangent_ref[...], weight_ref[...]).astype(bf16)
    inner[...] = dot(band_t[TILE : TILE + SLOTS, :], grad_mix)
    copy = pltpu.make_async_copy(inner, inner_hbm, sem)
    copy.start()
    low_ref[...] = dot(band_t[:TILE, :], grad_mix).astype(bf16)
    high_ref[...] = dot(band_t[TILE + SLOTS :, :], grad_mix).astype(bf16)
    copy.wait()


def spread(columns, counts, values, cotangent, weight):
    return pl.pallas_call(
        spread_kernel,
        out_shape=(
            jax.ShapeDtypeStruct((TILE, D), bf16),
            jax.ShapeDtypeStruct((TILE, D), bf16),
            jax.ShapeDtypeStruct((SLOTS, D), f32),
        ),
        in_specs=[SMEM, SMEM, VMEM, VMEM, VMEM],
        out_specs=(VMEM, VMEM, ANY),
        scratch_shapes=[
            pltpu.VMEM((2 * SLOTS, SLOTS), bf16),
            pltpu.VMEM((SLOTS, D), f32),
            pltpu.SemaphoreType.DMA,
        ],
        compiler_params=params(63.9),
        cost_estimate=cost(10**9, 5 * 2**20),
        name="spread",
    )(columns, counts, values, cotangent, weight)


def prepare_kernel(
    columns_ref,
    count_ref,
    values_ref,
    order_ref,
    mix_hbm,
    mix_t_hbm,
    band_ref,
    band_t,
    mix,
    mix_t,
    sems,
):
    fill_band(columns_ref, count_ref, values_ref, band_ref, False)
    fill_band(columns_ref, count_ref, values_ref, band_t, True)

    def place(column, u):
        peer, slot = column >> 3, column & 3
        halo = jnp.where(peer < PEERS // 2, 2 * SLOTS - TILE, -PEERS) + 2 * peer + slot - 2
        source = jnp.where(slot < 2, TILE + 2 * peer + slot, halo)
        return jnp.where(((column >> 2) & 1) == u, source, -1)

    shape = (2 * SLOTS, ROWS)
    for u in range(2):
        moved = jnp.where(iota(shape, 0) == place(iota((1, ROWS), 1), u), 1.0, 0.0)
        mix[u * SLOTS : (u + 1) * SLOTS, :] = dot(band_ref[...], moved.astype(bf16)).astype(bf16)
        back = jnp.where(iota(shape[::-1], 1) == place(iota((ROWS, 1), 0), u), 1.0, 0.0)
        mix_t[:, u * SLOTS : (u + 1) * SLOTS] = dot(back.astype(bf16), band_t[...]).astype(bf16)
    copies = [
        pltpu.make_async_copy(mix, mix_hbm, sems.at[0]),
        pltpu.make_async_copy(mix_t, mix_t_hbm, sems.at[1]),
    ]
    for copy in copies:
        copy.start()
    for copy in copies:
        copy.wait()


def prepare(columns, counts, values, order):
    return pl.pallas_call(
        prepare_kernel,
        out_shape=(
            jax.ShapeDtypeStruct((2 * SLOTS, ROWS), bf16),
            jax.ShapeDtypeStruct((ROWS, 2 * SLOTS), bf16),
            jax.ShapeDtypeStruct((SLOTS, 2 * SLOTS), bf16),
        ),
        in_specs=[SMEM, SMEM, VMEM, ANY],
        out_specs=(ANY, ANY, VMEM),
        scratch_shapes=[
            pltpu.VMEM((2 * SLOTS, SLOTS), bf16),
            pltpu.VMEM((2 * SLOTS, ROWS), bf16),
            pltpu.VMEM((ROWS, 2 * SLOTS), bf16),
            pltpu.SemaphoreType.DMA((2,)),
        ],
        compiler_params=params(63.9),
        cost_estimate=cost(10**9, 4 * 2**20),
        name="prepare",
    )(columns, counts, values, order)


def middle_kernel(
    rows_hbm,
    mix_hbm,
    weight_hbm,
    inner_hbm,
    left_hbm,
    right_hbm,
    mix_t_hbm,
    top_hbm,
    bottom_hbm,
    out_hbm,
    acts,
    out,
    rows,
    mix,
    weight,
    inner,
    left,
    right,
    mix_t,
    sems,
    act_sems,
    out_sems,
):
    pairs = (
        (mix_hbm, mix),
        (rows_hbm, rows),
        (weight_hbm, weight),
        (inner_hbm, inner),
        (left_hbm, left),
        (right_hbm, right),
        (mix_t_hbm, mix_t),
    )
    copies = [pltpu.make_async_copy(a, b, sems.at[i]) for i, (a, b) in enumerate(pairs)]
    for copy in copies:
        copy.start()
    copies[0].wait()
    copies[1].wait()
    halves = dot(mix[...], rows[...]).astype(bf16)
    mixed = jnp.concatenate([halves[:SLOTS], halves[SLOTS:]], axis=1)
    copies[2].wait()
    before = dot(mixed, weight[...])
    erf = 0.5 * (1.0 + lax.erf(before * ROOT_HALF))
    acted = (before * erf).astype(bf16)
    acts[...] = acted
    act_copies = [
        pltpu.make_async_copy(acts.at[pl.ds(i * TILE, TILE), :], to, act_sems.at[i])
        for i, to in enumerate((top_hbm, bottom_hbm))
    ]
    for copy in act_copies:
        copy.start()
    slope = erf + before * (INV_ROOT_TAU * jnp.exp(-0.5 * before * before))
    for copy in copies[3:6]:
        copy.wait()
    rims = jnp.concatenate([left[...], right[...]], axis=0).astype(f32)
    grad_before = ((inner[...] + rims) * slope).astype(bf16)
    grad_mix = dot_t(grad_before, weight[...]).astype(bf16)
    stacked = jnp.concatenate([grad_mix[:, :HALF], grad_mix[:, HALF:]], axis=0)
    copies[6].wait()
    send_rows(lambda r: dot(mix_t[r, :], stacked), out, out_hbm, out_sems)
    for copy in act_copies:
        copy.wait()


def middle(*arrays):
    return pl.pallas_call(
        middle_kernel,
        out_shape=(
            jax.ShapeDtypeStruct((TILE, D), bf16),
            jax.ShapeDtypeStruct((TILE, D), bf16),
            jax.ShapeDtypeStruct((ROWS, HALF), bf16),
        ),
        in_specs=[ANY] * 7,
        out_specs=(ANY,) * 3,
        scratch_shapes=[pltpu.VMEM((SLOTS, D), bf16), pltpu.VMEM((ROWS, HALF), bf16)]
        + [pltpu.VMEM(a.shape, a.dtype) for a in arrays]
        + [pltpu.SemaphoreType.DMA((n,)) for n in (7, 2, PIECES)],
        compiler_params=params(63.9),
        cost_estimate=cost(3 * 10**9, 8 * 2**20),
        name="middle",
    )(*arrays)


def finish_kernel(left_hbm, top_hbm, bottom_hbm, right_hbm, band_hbm, weight_hbm, out_ref, wide, band, weight, sems):
    sources = (left_hbm, top_hbm, bottom_hbm, right_hbm)
    copies = [
        pltpu.make_async_copy(a, wide.at[pl.ds(i * TILE, TILE), :], sems.at[i])
        for i, a in enumerate(sources)
    ]
    copies.append(pltpu.make_async_copy(band_hbm, band, sems.at[4]))
    copies.append(pltpu.make_async_copy(weight_hbm, weight, sems.at[5]))
    for copy in copies:
        copy.start()
    for copy in copies[:5]:
        copy.wait()
    mixed = dot(band[...], wide[...]).astype(bf16)
    copies[5].wait()
    out_ref[...] = dot(mixed, weight[...]).astype(bf16)


def finish(*arrays):
    return pl.pallas_call(
        finish_kernel,
        out_shape=jax.ShapeDtypeStruct((SLOTS, D), bf16),
        in_specs=[ANY] * 6,
        out_specs=VMEM,
        scratch_shapes=[
            pltpu.VMEM((2 * SLOTS, D), bf16),
            pltpu.VMEM((SLOTS, 2 * SLOTS), bf16),
            pltpu.VMEM((D, D), bf16),
            pltpu.SemaphoreType.DMA((6,)),
        ],
        compiler_params=params(16),
        cost_estimate=cost(10**9, 5 * 2**20),
        name="finish",
    )(*arrays)


def gather_kernel(target_ref, rows_ref, out_ref, pick):
    diagonal = iota((NODES, NPAD), 0) == iota((NODES, NPAD), 1)
    own_row = jnp.sum(jnp.where(diagonal, target_ref[0:1, :], 0), axis=1, keepdims=True)
    halo_row = jnp.sum(jnp.where(diagonal, target_ref[1:2, :], 0), axis=1, keepdims=True)
    lanes = iota((NODES, ROWS), 1)
    for u in range(2):
        hit = (lanes - 4 * u == own_row) | (lanes - 4 * u == halo_row)
        pick[u * NODES : (u + 1) * NODES, :] = jnp.where(hit, 1.0, 0.0).astype(bf16)
    for u in range(2):
        picked = dot(pick[u * NODES : (u + 1) * NODES, :], rows_ref[...])
        out_ref[:, u * HALF : (u + 1) * HALF] = picked.astype(bf16)


def gather(target, rows):
    return pl.pallas_call(
        gather_kernel,
        out_shape=jax.ShapeDtypeStruct((NODES, D), bf16),
        in_specs=[VMEM, VMEM],
        out_specs=VMEM,
        scratch_shapes=[pltpu.VMEM((2 * NODES, ROWS), bf16)],
        compiler_params=params(16),
        cost_estimate=cost(4 * 10**8, 2 * 2**20),
        name="gather",
    )(target, rows)


def swap(rows):
    return lax.all_to_all(
        rows.reshape(PEERS, 8, HALF), ("enc", "dom"), split_axis=0, concat_axis=0, tiled=True
    ).reshape(ROWS, HALF)


def local(
    token_states,
    token_nodes,
    expand_weight,
    contract_weight,
    node_owner,
    tile_columns,
    tile_count,
    tile_values,
    first_weight,
    second_weight,
    output_cotangent,
):
    device = lax.axis_index("enc") * GROUP + lax.axis_index("dom")
    upper = (device >= PEERS // 2).astype(jnp.int32).reshape(1)
    rightward = [(i, i + 1) for i in range(GROUP - 1)]
    leftward = [(i + 1, i) for i in range(GROUP - 1)]
    outgoing, target = encode(
        upper, node_owner.reshape(1, NODES), token_nodes, token_states, expand_weight, contract_weight
    )
    arrived = swap(outgoing)
    target, later_cotangent = lax.optimization_barrier((target, output_cotangent))
    low, high, inner = spread(tile_columns, tile_count, tile_values, later_cotangent, second_weight)
    mix, mix_t, band = prepare(tile_columns, tile_count, tile_values, inner)
    from_right = lax.ppermute(low, "dom", leftward)
    from_left = lax.ppermute(high, "dom", rightward)
    top, bottom, grads = middle(arrived, mix, first_weight, inner, from_left, from_right, mix_t)
    returned = swap(grads)
    left = lax.ppermute(bottom, "dom", rightward)
    right = lax.ppermute(top, "dom", leftward)
    graph_output = finish(left, top, bottom, right, band, second_weight)
    return (graph_output, gather(target, returned))


def solution(mesh):
    rows = ("enc", "dom")
    placed = (
        P(rows, None),
        P(rows, None),
        P(),
        P(),
        P(rows, None),
        P(rows, None, None),
        P(rows, None),
        P(rows, None, None, None, None),
        P(),
        P(),
        P(rows, None),
    )
    return jax.shard_map(
        local,
        mesh=mesh,
        in_specs=placed,
        out_specs=(P(rows, None), P(rows, None)),
        check_vma=False,
    )
```

```python
import jax
import jax.numpy as jnp
from jax import lax
from jax.experimental import pallas as pl
from jax.experimental.pallas import tpu as pltpu
from jax.sharding import PartitionSpec as P

NODES = 192
NPAD = 256
TOKENS = 1024
D = 1024
FF = 4096
HALF = 512
PEERS = 128
GROUP = 8
ROWS = 1024
TILE = 128
SLOTS = 256

CHUNK = 512
CHUNKS = FF // CHUNK
BLOCK = 512
BLOCKS = TOKENS // BLOCK
AHEAD = 2
PIECES = 4

bf16 = jnp.bfloat16
f32 = jnp.float32
EPS = 1e-07
ROOT_HALF = 0.7071067811865476
INV_ROOT_TAU = 0.3989422804014327

ANY = pl.BlockSpec(memory_space=pl.ANY)
VMEM = pl.BlockSpec(memory_space=pltpu.VMEM)
SMEM = pl.BlockSpec(memory_space=pltpu.SMEM)


def dot(a, b):
    return jnp.dot(a, b, preferred_element_type=f32)


def dot_t(a, b):
    return lax.dot_general(a, b, (((1,), (1,)), ((), ())), preferred_element_type=f32)


def iota(shape, dim):
    return lax.broadcasted_iota(jnp.int32, shape, dim)


def params(mib):
    return pltpu.CompilerParams(vmem_limit_bytes=int(mib * 2**20))


def cost(flops, moved):
    return pl.CostEstimate(flops=flops, bytes_accessed=moved, transcendentals=0)


def send_rows(rows_of, out, out_hbm, sem):
    size = ROWS // PIECES
    copies = []
    for i in range(PIECES):
        rows = pl.ds(i * size, size)
        out[rows, :] = rows_of(rows).astype(bf16)
        copies.append(pltpu.make_async_copy(out.at[rows, :], out_hbm.at[rows, :], sem.at[i]))
        copies[-1].start()
    for copy in copies:
        copy.wait()


def encode_kernel(
    upper_ref,
    owner_ref,
    node_ref,
    states_hbm,
    expand_hbm,
    contract_hbm,
    out_hbm,
    target_ref,
    out,
    states,
    expand,
    contract,
    total,
    hidden_a,
    hidden_b,
    owner_pad,
    route,
    member,
    normed,
    state_sem,
    expand_sem,
    contract_sem,
    out_sem,
):
    def block_of(m):
        return pl.ds(m * BLOCK, BLOCK)

    def chunk_of(c):
        return pl.ds(pl.multiple_of(c * CHUNK, CHUNK), CHUNK)

    def start_expand(c):
        pltpu.make_async_copy(
            expand_hbm.at[:, chunk_of(c)], expand.at[c], expand_sem.at[c]
        ).start()

    def start(c):
        if not isinstance(c, int) or c > 0:
            start_expand(c)
        pltpu.make_async_copy(
            contract_hbm.at[chunk_of(c), :], contract.at[c], contract_sem.at[c]
        ).start()

    def wait_expand(c):
        pltpu.make_async_copy(
            expand_hbm.at[:, chunk_of(c)], expand.at[c], expand_sem.at[c]
        ).wait()

    def wait(c):
        if not isinstance(c, int) or c > 0:
            wait_expand(c)
        pltpu.make_async_copy(
            contract_hbm.at[chunk_of(c), :], contract.at[c], contract_sem.at[c]
        ).wait()

    def state_copy(m):
        return pltpu.make_async_copy(
            states_hbm.at[block_of(m), :], states.at[block_of(m), :], state_sem.at[m]
        )

    state_copy(0).start()
    start_expand(0)
    for m in range(1, BLOCKS):
        state_copy(m).start()
    start(0)

    owner_pad[...] = jnp.full((8, NPAD), -4096, jnp.int32)
    owner_pad[0:1, 0:NODES] = owner_ref[...]
    owner = owner_pad[0:1, :]
    named = jnp.where(iota((PEERS, NPAD), 0) == owner, 1.0, 0.0).astype(bf16)
    before = jnp.where(iota((NPAD, NPAD), 0) < iota((NPAD, NPAD), 1), 1.0, 0.0).astype(bf16)
    earlier = dot(named, before)
    rank = jnp.sum(named.astype(f32) * earlier, axis=0, keepdims=True).astype(jnp.int32)
    own_row = owner * 8 + rank
    upper = upper_ref[0]
    beside = owner + jnp.where(upper == 1, 1, -1)
    edge = jnp.where(upper == 1, GROUP - 1, 0)
    has_beside = (owner & (GROUP - 1)) != edge
    halo_row = jnp.where(has_beside, beside * 8 + 2 + rank, -4096)
    target_ref[...] = jnp.where(iota((8, NPAD), 0) == 0, own_row, halo_row)
    rows = iota((ROWS, NPAD), 0)
    for u in range(2):
        shifted = rows - 4 * u
        hit = (shifted == own_row) | (shifted == halo_row)
        route[:, u * NPAD : (u + 1) * NPAD] = jnp.where(hit, 1.0, 0.0).astype(bf16)
    mask = jnp.where(iota((NPAD, TOKENS), 0) == node_ref[...], 1.0, 0.0)
    member[...] = mask.astype(bf16)
    counts = jnp.maximum(jnp.sum(mask, axis=1, keepdims=True), 1.0)


    def first(c, m):
        return dot(states[block_of(m), :], expand[c])

    def second(c, m, values, opening):
        acted = 0.5 * values * (1.0 + lax.erf(values * ROOT_HALF))
        product = dot(acted.astype(bf16), contract[c])
        total[block_of(m), :] = product if opening else total[block_of(m), :] + product

    buffers = (hidden_a, hidden_b)

    def step(c, opening=False, closing=False):
        for m in range(BLOCKS):
            now, later = buffers[m % 2], buffers[(m + 1) % 2]
            if m + 1 < BLOCKS:
                later[...] = first(c, m + 1)
            elif not closing:
                if opening:
                    start(2)
                    wait(1)
                later[...] = first(c + 1, 0)
            second(c, m, now[...], opening)
            if closing:
                settle(m)

    def settle(m):
        mixed = total[block_of(m), :] + states[block_of(m), :].astype(f32)
        centred = mixed - jnp.mean(mixed, axis=1, keepdims=True)
        variance = jnp.mean(centred * centred, axis=1, keepdims=True)
        normed[block_of(m), :] = (centred * lax.rsqrt(variance + EPS)).astype(bf16)

    state_copy(0).wait()
    wait_expand(0)
    start(1)
    hidden_a[...] = first(0, 0)
    for m in range(1, BLOCKS):
        state_copy(m).wait()
    wait(0)
    step(0, opening=True)

    def middle_step(c, carry):
        @pl.when(c + AHEAD < CHUNKS)
        def _():
            start(c + AHEAD)

        wait(c + 1)
        step(c)
        return carry

    lax.fori_loop(1, CHUNKS - 1, middle_step, 0)
    step(CHUNKS - 1, closing=True)
    summed = dot(member[...], normed[...])
    embeds = (summed / counts).astype(bf16)
    stacked = jnp.concatenate([embeds[:, :HALF], embeds[:, HALF:]], axis=0)
    send_rows(lambda r: dot(route[r, :], stacked), out, out_hbm, out_sem)


def encode(upper, owner, node_ids, states, expand_weight, contract_weight):
    dma = pltpu.SemaphoreType.DMA
    return pl.pallas_call(
        encode_kernel,
        out_shape=(
            jax.ShapeDtypeStruct((ROWS, HALF), bf16),
            jax.ShapeDtypeStruct((8, NPAD), jnp.int32),
        ),
        in_specs=[SMEM, VMEM, VMEM, ANY, ANY, ANY],
        out_specs=(ANY, VMEM),
        scratch_shapes=[
            pltpu.VMEM((ROWS, HALF), bf16),
            pltpu.VMEM((TOKENS, D), bf16),
            pltpu.VMEM((CHUNKS, D, CHUNK), bf16),
            pltpu.VMEM((CHUNKS, CHUNK, D), bf16),
            pltpu.VMEM((TOKENS, D), f32),
            pltpu.VMEM((BLOCK, CHUNK), f32),
            pltpu.VMEM((BLOCK, CHUNK), f32),
            pltpu.VMEM((8, NPAD), jnp.int32),
            pltpu.VMEM((ROWS, 2 * NPAD), bf16),
            pltpu.VMEM((NPAD, TOKENS), bf16),
            pltpu.VMEM((TOKENS, D), bf16),
            dma((BLOCKS,)),
            dma((CHUNKS,)),
            dma((CHUNKS,)),
            dma((PIECES,)),
        ],
        compiler_params=params(56),
        cost_estimate=cost(4 * TOKENS * D * FF, 20 * 2**20),
        name="encode",
    )(upper, owner, node_ids, states, expand_weight, contract_weight)


def fill_band(columns_ref, count_ref, values_ref, band, transposed):
    band[...] = jnp.zeros(band.shape, bf16)
    for r in range(2):
        for c in range(r, r + 3):
            tile = jnp.zeros((TILE, TILE), f32)
            for s in range(3):
                used = (s < count_ref[0, r]) & (columns_ref[0, r, s] == c)
                tile += jnp.where(used, 1.0, 0.0) * values_ref[0, r, s].astype(f32)
            rows, lanes = slice(r * TILE, (r + 1) * TILE), slice(c * TILE, (c + 1) * TILE)
            if transposed:
                band[lanes, rows] = tile.T.astype(bf16)
            else:
                band[rows, lanes] = tile.astype(bf16)


def spread_kernel(
    columns_ref, count_ref, values_ref, cotangent_ref, weight_ref, low_ref, high_ref, inner_hbm, band_t, inner, sem
):
    fill_band(columns_ref, count_ref, values_ref, band_t, True)
    grad_mix = dot_t(cotangent_ref[...], weight_ref[...]).astype(bf16)
    inner[...] = dot(band_t[TILE : TILE + SLOTS, :], grad_mix)
    copy = pltpu.make_async_copy(inner, inner_hbm, sem)
    copy.start()
    low_ref[...] = dot(band_t[:TILE, :], grad_mix).astype(bf16)
    high_ref[...] = dot(band_t[TILE + SLOTS :, :], grad_mix).astype(bf16)
    copy.wait()


def spread(columns, counts, values, cotangent, weight):
    return pl.pallas_call(
        spread_kernel,
        out_shape=(
            jax.ShapeDtypeStruct((TILE, D), bf16),
            jax.ShapeDtypeStruct((TILE, D), bf16),
            jax.ShapeDtypeStruct((SLOTS, D), f32),
        ),
        in_specs=[SMEM, SMEM, VMEM, VMEM, VMEM],
        out_specs=(VMEM, VMEM, ANY),
        scratch_shapes=[
            pltpu.VMEM((2 * SLOTS, SLOTS), bf16),
            pltpu.VMEM((SLOTS, D), f32),
            pltpu.SemaphoreType.DMA,
        ],
        compiler_params=params(63.9),
        cost_estimate=cost(10**9, 5 * 2**20),
        name="spread",
    )(columns, counts, values, cotangent, weight)


def prepare_kernel(
    columns_ref,
    count_ref,
    values_ref,
    order_ref,
    mix_hbm,
    mix_t_hbm,
    band_ref,
    band_t,
    mix,
    mix_t,
    sems,
):
    fill_band(columns_ref, count_ref, values_ref, band_ref, False)
    fill_band(columns_ref, count_ref, values_ref, band_t, True)

    def place(column, u):
        peer, slot = column >> 3, column & 3
        halo = jnp.where(peer < PEERS // 2, 2 * SLOTS - TILE, -PEERS) + 2 * peer + slot - 2
        source = jnp.where(slot < 2, TILE + 2 * peer + slot, halo)
        return jnp.where(((column >> 2) & 1) == u, source, -1)

    shape = (2 * SLOTS, ROWS)
    for u in range(2):
        moved = jnp.where(iota(shape, 0) == place(iota((1, ROWS), 1), u), 1.0, 0.0)
        mix[u * SLOTS : (u + 1) * SLOTS, :] = dot(band_ref[...], moved.astype(bf16)).astype(bf16)
        back = jnp.where(iota(shape[::-1], 1) == place(iota((ROWS, 1), 0), u), 1.0, 0.0)
        mix_t[:, u * SLOTS : (u + 1) * SLOTS] = dot(back.astype(bf16), band_t[...]).astype(bf16)
    copies = [
        pltpu.make_async_copy(mix, mix_hbm, sems.at[0]),
        pltpu.make_async_copy(mix_t, mix_t_hbm, sems.at[1]),
    ]
    for copy in copies:
        copy.start()
    for copy in copies:
        copy.wait()


def prepare(columns, counts, values, order):
    return pl.pallas_call(
        prepare_kernel,
        out_shape=(
            jax.ShapeDtypeStruct((2 * SLOTS, ROWS), bf16),
            jax.ShapeDtypeStruct((ROWS, 2 * SLOTS), bf16),
            jax.ShapeDtypeStruct((SLOTS, 2 * SLOTS), bf16),
        ),
        in_specs=[SMEM, SMEM, VMEM, ANY],
        out_specs=(ANY, ANY, VMEM),
        scratch_shapes=[
            pltpu.VMEM((2 * SLOTS, SLOTS), bf16),
            pltpu.VMEM((2 * SLOTS, ROWS), bf16),
            pltpu.VMEM((ROWS, 2 * SLOTS), bf16),
            pltpu.SemaphoreType.DMA((2,)),
        ],
        compiler_params=params(63.9),
        cost_estimate=cost(10**9, 4 * 2**20),
        name="prepare",
    )(columns, counts, values, order)


def middle_kernel(
    rows_hbm,
    mix_hbm,
    weight_hbm,
    inner_hbm,
    left_hbm,
    right_hbm,
    mix_t_hbm,
    top_hbm,
    bottom_hbm,
    out_hbm,
    acts,
    out,
    rows,
    mix,
    weight,
    inner,
    left,
    right,
    mix_t,
    sems,
    act_sems,
    out_sems,
):
    pairs = (
        (mix_hbm, mix),
        (rows_hbm, rows),
        (weight_hbm, weight),
        (inner_hbm, inner),
        (left_hbm, left),
        (right_hbm, right),
        (mix_t_hbm, mix_t),
    )
    copies = [pltpu.make_async_copy(a, b, sems.at[i]) for i, (a, b) in enumerate(pairs)]
    for copy in copies:
        copy.start()
    copies[0].wait()
    copies[1].wait()
    halves = dot(mix[...], rows[...]).astype(bf16)
    mixed = jnp.concatenate([halves[:SLOTS], halves[SLOTS:]], axis=1)
    copies[2].wait()
    before = dot(mixed, weight[...])
    erf = 0.5 * (1.0 + lax.erf(before * ROOT_HALF))
    acted = (before * erf).astype(bf16)
    acts[...] = acted
    act_copies = [
        pltpu.make_async_copy(acts.at[pl.ds(i * TILE, TILE), :], to, act_sems.at[i])
        for i, to in enumerate((top_hbm, bottom_hbm))
    ]
    for copy in act_copies:
        copy.start()
    slope = erf + before * (INV_ROOT_TAU * jnp.exp(-0.5 * before * before))
    for copy in copies[3:6]:
        copy.wait()
    rims = jnp.concatenate([left[...], right[...]], axis=0).astype(f32)
    grad_before = ((inner[...] + rims) * slope).astype(bf16)
    grad_mix = dot_t(grad_before, weight[...]).astype(bf16)
    stacked = jnp.concatenate([grad_mix[:, :HALF], grad_mix[:, HALF:]], axis=0)
    copies[6].wait()
    send_rows(lambda r: dot(mix_t[r, :], stacked), out, out_hbm, out_sems)
    for copy in act_copies:
        copy.wait()


def middle(*arrays):
    return pl.pallas_call(
        middle_kernel,
        out_shape=(
            jax.ShapeDtypeStruct((TILE, D), bf16),
            jax.ShapeDtypeStruct((TILE, D), bf16),
            jax.ShapeDtypeStruct((ROWS, HALF), bf16),
        ),
        in_specs=[ANY] * 7,
        out_specs=(ANY,) * 3,
        scratch_shapes=[pltpu.VMEM((SLOTS, D), bf16), pltpu.VMEM((ROWS, HALF), bf16)]
        + [pltpu.VMEM(a.shape, a.dtype) for a in arrays]
        + [pltpu.SemaphoreType.DMA((n,)) for n in (7, 2, PIECES)],
        compiler_params=params(63.9),
        cost_estimate=cost(3 * 10**9, 8 * 2**20),
        name="middle",
    )(*arrays)


def own_part_kernel(
    top_hbm, bottom_hbm, band_hbm, part_ref, first_ref, last_ref, acts, band, sems
):
    copies = [
        pltpu.make_async_copy(top_hbm, acts.at[pl.ds(0, TILE), :], sems.at[0]),
        pltpu.make_async_copy(bottom_hbm, acts.at[pl.ds(TILE, TILE), :], sems.at[1]),
        pltpu.make_async_copy(band_hbm, band, sems.at[2]),
    ]
    for copy in copies:
        copy.start()
    for copy in copies:
        copy.wait()
    part_ref[...] = dot(band[:, TILE : TILE + SLOTS], acts[...])
    first_ref[...] = band[:, :TILE]
    last_ref[...] = band[:, TILE + SLOTS :]


def own_part(*arrays):
    return pl.pallas_call(
        own_part_kernel,
        out_shape=(
            jax.ShapeDtypeStruct((SLOTS, D), f32),
            jax.ShapeDtypeStruct((SLOTS, TILE), bf16),
            jax.ShapeDtypeStruct((SLOTS, TILE), bf16),
        ),
        in_specs=[ANY] * 3,
        out_specs=(VMEM,) * 3,
        scratch_shapes=[
            pltpu.VMEM((SLOTS, D), bf16),
            pltpu.VMEM((SLOTS, 2 * SLOTS), bf16),
            pltpu.SemaphoreType.DMA((3,)),
        ],
        compiler_params=params(16),
        cost_estimate=cost(2 * 10**8, 3 * 2**20),
        name="own_part",
    )(*arrays)


def finish_kernel(part_ref, first_ref, last_ref, left_ref, right_ref, weight_ref, out_ref):
    mixed = part_ref[...] + dot(first_ref[...], left_ref[...]) + dot(last_ref[...], right_ref[...])
    out_ref[...] = dot(mixed.astype(bf16), weight_ref[...]).astype(bf16)


def finish(*arrays):
    return pl.pallas_call(
        finish_kernel,
        out_shape=jax.ShapeDtypeStruct((SLOTS, D), bf16),
        in_specs=[VMEM] * 6,
        out_specs=VMEM,
        compiler_params=params(16),
        cost_estimate=cost(10**9, 5 * 2**20),
        name="finish",
    )(*arrays)


def gather_kernel(target_ref, rows_ref, out_ref, pick):
    diagonal = iota((NODES, NPAD), 0) == iota((NODES, NPAD), 1)
    own_row = jnp.sum(jnp.where(diagonal, target_ref[0:1, :], 0), axis=1, keepdims=True)
    halo_row = jnp.sum(jnp.where(diagonal, target_ref[1:2, :], 0), axis=1, keepdims=True)
    lanes = iota((NODES, ROWS), 1)
    for u in range(2):
        hit = (lanes - 4 * u == own_row) | (lanes - 4 * u == halo_row)
        pick[u * NODES : (u + 1) * NODES, :] = jnp.where(hit, 1.0, 0.0).astype(bf16)
    for u in range(2):
        picked = dot(pick[u * NODES : (u + 1) * NODES, :], rows_ref[...])
        out_ref[:, u * HALF : (u + 1) * HALF] = picked.astype(bf16)


def gather(target, rows):
    return pl.pallas_call(
        gather_kernel,
        out_shape=jax.ShapeDtypeStruct((NODES, D), bf16),
        in_specs=[VMEM, VMEM],
        out_specs=VMEM,
        scratch_shapes=[pltpu.VMEM((2 * NODES, ROWS), bf16)],
        compiler_params=params(16),
        cost_estimate=cost(4 * 10**8, 2 * 2**20),
        name="gather",
    )(target, rows)


def swap(rows):
    return lax.all_to_all(
        rows.reshape(PEERS, 8, HALF), ("enc", "dom"), split_axis=0, concat_axis=0, tiled=True
    ).reshape(ROWS, HALF)


def local(
    token_states,
    token_nodes,
    expand_weight,
    contract_weight,
    node_owner,
    tile_columns,
    tile_count,
    tile_values,
    first_weight,
    second_weight,
    output_cotangent,
):
    device = lax.axis_index("enc") * GROUP + lax.axis_index("dom")
    upper = (device >= PEERS // 2).astype(jnp.int32).reshape(1)
    rightward = [(i, i + 1) for i in range(GROUP - 1)]
    leftward = [(i + 1, i) for i in range(GROUP - 1)]
    outgoing, target = encode(
        upper, node_owner.reshape(1, NODES), token_nodes, token_states, expand_weight, contract_weight
    )
    arrived = swap(outgoing)
    target, later_cotangent = lax.optimization_barrier((target, output_cotangent))
    low, high, inner = spread(tile_columns, tile_count, tile_values, later_cotangent, second_weight)
    mix, mix_t, band = prepare(tile_columns, tile_count, tile_values, inner)
    from_right = lax.ppermute(low, "dom", leftward)
    from_left = lax.ppermute(high, "dom", rightward)
    top, bottom, grads = middle(arrived, mix, first_weight, inner, from_left, from_right, mix_t)
    returned = swap(grads)
    left = lax.ppermute(bottom, "dom", rightward)
    right = lax.ppermute(top, "dom", leftward)
    part, first, last = own_part(top, bottom, band)
    graph_output = finish(part, first, last, left, right, second_weight)
    return (graph_output, gather(target, returned))


def solution(mesh):
    rows = ("enc", "dom")
    placed = (
        P(rows, None),
        P(rows, None),
        P(),
        P(),
        P(rows, None),
        P(rows, None, None),
        P(rows, None),
        P(rows, None, None, None, None),
        P(),
        P(),
        P(rows, None),
    )
    return jax.shard_map(
        local,
        mesh=mesh,
        in_specs=placed,
        out_specs=(P(rows, None), P(rows, None)),
        check_vma=False,
    )
```

```python
import jax
import jax.numpy as jnp
from jax import lax
from jax.experimental import pallas as pl
from jax.experimental.pallas import tpu as pltpu
from jax.sharding import PartitionSpec as P

NODES = 192
NPAD = 256
TOKENS = 1024
D = 1024
FF = 4096
HALF = 512
PEERS = 128
GROUP = 8
ROWS = 1024
TILE = 128
SLOTS = 256

CHUNK = 512
CHUNKS = FF // CHUNK
BLOCK = 512
BLOCKS = TOKENS // BLOCK
AHEAD = 2
OPEN = (512, 512)
USUAL = (512, 512)
CLOSE = (256, 256, 256, 256)
PIECES = 4

bf16 = jnp.bfloat16
f32 = jnp.float32
EPS = 1e-07
ROOT_HALF = 0.7071067811865476
INV_ROOT_TAU = 0.3989422804014327

ANY = pl.BlockSpec(memory_space=pl.ANY)
VMEM = pl.BlockSpec(memory_space=pltpu.VMEM)
SMEM = pl.BlockSpec(memory_space=pltpu.SMEM)


def dot(a, b):
    return jnp.dot(a, b, preferred_element_type=f32)


def dot_t(a, b):
    return lax.dot_general(a, b, (((1,), (1,)), ((), ())), preferred_element_type=f32)


def iota(shape, dim):
    return lax.broadcasted_iota(jnp.int32, shape, dim)


def params(mib):
    return pltpu.CompilerParams(vmem_limit_bytes=int(mib * 2**20))


def cost(flops, moved):
    return pl.CostEstimate(flops=flops, bytes_accessed=moved, transcendentals=0)


def send_rows(rows_of, out, out_hbm, sem):
    size = ROWS // PIECES
    copies = []
    for i in range(PIECES):
        rows = pl.ds(i * size, size)
        out[rows, :] = rows_of(rows).astype(bf16)
        copies.append(pltpu.make_async_copy(out.at[rows, :], out_hbm.at[rows, :], sem.at[i]))
        copies[-1].start()
    for copy in copies:
        copy.wait()


def encode_kernel(
    upper_ref,
    owner_ref,
    node_ref,
    states_hbm,
    expand_hbm,
    contract_hbm,
    out_hbm,
    target_ref,
    out,
    states,
    expand,
    contract,
    total,
    hidden_a,
    hidden_b,
    owner_pad,
    route,
    member,
    normed,
    state_sem,
    expand_sem,
    contract_sem,
    out_sem,
):
    def block_of(m):
        return pl.ds(m * BLOCK, BLOCK)

    def chunk_of(c):
        return pl.ds(pl.multiple_of(c * CHUNK, CHUNK), CHUNK)

    def start_expand(c):
        pltpu.make_async_copy(
            expand_hbm.at[:, chunk_of(c)], expand.at[c], expand_sem.at[c]
        ).start()

    def start(c):
        if not isinstance(c, int) or c > 0:
            start_expand(c)
        pltpu.make_async_copy(
            contract_hbm.at[chunk_of(c), :], contract.at[c], contract_sem.at[c]
        ).start()

    def wait_expand(c):
        pltpu.make_async_copy(
            expand_hbm.at[:, chunk_of(c)], expand.at[c], expand_sem.at[c]
        ).wait()

    def wait(c):
        if not isinstance(c, int) or c > 0:
            wait_expand(c)
        pltpu.make_async_copy(
            contract_hbm.at[chunk_of(c), :], contract.at[c], contract_sem.at[c]
        ).wait()

    def state_copy(m):
        return pltpu.make_async_copy(
            states_hbm.at[block_of(m), :], states.at[block_of(m), :], state_sem.at[m]
        )

    state_copy(0).start()
    start_expand(0)
    for m in range(1, BLOCKS):
        state_copy(m).start()
    start(0)

    owner_pad[...] = jnp.full((8, NPAD), -4096, jnp.int32)
    owner_pad[0:1, 0:NODES] = owner_ref[...]
    owner = owner_pad[0:1, :]
    named = jnp.where(iota((PEERS, NPAD), 0) == owner, 1.0, 0.0).astype(bf16)
    before = jnp.where(iota((NPAD, NPAD), 0) < iota((NPAD, NPAD), 1), 1.0, 0.0).astype(bf16)
    earlier = dot(named, before)
    rank = jnp.sum(named.astype(f32) * earlier, axis=0, keepdims=True).astype(jnp.int32)
    own_row = owner * 8 + rank
    upper = upper_ref[0]
    beside = owner + jnp.where(upper == 1, 1, -1)
    edge = jnp.where(upper == 1, GROUP - 1, 0)
    has_beside = (owner & (GROUP - 1)) != edge
    halo_row = jnp.where(has_beside, beside * 8 + 2 + rank, -4096)
    target_ref[...] = jnp.where(iota((8, NPAD), 0) == 0, own_row, halo_row)
    rows = iota((ROWS, NPAD), 0)
    for u in range(2):
        shifted = rows - 4 * u
        hit = (shifted == own_row) | (shifted == halo_row)
        route[:, u * NPAD : (u + 1) * NPAD] = jnp.where(hit, 1.0, 0.0).astype(bf16)
    mask = jnp.where(iota((NPAD, TOKENS), 0) == node_ref[...], 1.0, 0.0)
    member[...] = mask.astype(bf16)
    counts = jnp.maximum(jnp.sum(mask, axis=1, keepdims=True), 1.0)

    def first(c, r, n):
        return dot(states[pl.ds(r, n), :], expand[c])

    def second(c, r, n, values, opening):
        acted = 0.5 * values * (1.0 + lax.erf(values * ROOT_HALF))
        product = dot(acted.astype(bf16), contract[c])
        rows = pl.ds(r, n)
        total[rows, :] = product if opening else total[rows, :] + product

    buffers = (hidden_a, hidden_b)

    def step(c, sizes, following, opening=False, closing=False):
        starts = [sum(sizes[:k]) for k in range(len(sizes))]
        for k, (r, n) in enumerate(zip(starts, sizes)):
            now, later = buffers[k % 2], buffers[(k + 1) % 2]
            if k + 1 < len(sizes):
                later[: sizes[k + 1], :] = first(c, starts[k + 1], sizes[k + 1])
            elif not closing:
                if opening:
                    start(2)
                    wait(1)
                later[:following, :] = first(c + 1, 0, following)
            second(c, r, n, now[:n, :], opening)
            if closing:
                settle(pl.ds(r, n))

    def settle(rows):
        mixed = total[rows, :] + states[rows, :].astype(f32)
        centred = mixed - jnp.mean(mixed, axis=1, keepdims=True)
        variance = jnp.mean(centred * centred, axis=1, keepdims=True)
        normed[rows, :] = (centred * lax.rsqrt(variance + EPS)).astype(bf16)

    state_copy(0).wait()
    wait_expand(0)
    start(1)
    hidden_a[:OPEN[0], :] = first(0, 0, OPEN[0])
    for m in range(1, BLOCKS):
        state_copy(m).wait()
    wait(0)
    step(0, OPEN, USUAL[0], opening=True)

    def middle_step(c, carry):
        @pl.when(c + AHEAD < CHUNKS)
        def _():
            start(c + AHEAD)

        wait(c + 1)
        step(c, USUAL, USUAL[0])
        return carry

    lax.fori_loop(1, CHUNKS - 2, middle_step, 0)
    wait(CHUNKS - 1)
    step(CHUNKS - 2, USUAL, CLOSE[0])
    step(CHUNKS - 1, CLOSE, None, closing=True)
    summed = dot(member[...], normed[...])
    embeds = (summed / counts).astype(bf16)
    stacked = jnp.concatenate([embeds[:, :HALF], embeds[:, HALF:]], axis=0)
    send_rows(lambda r: dot(route[r, :], stacked), out, out_hbm, out_sem)


def encode(upper, owner, node_ids, states, expand_weight, contract_weight):
    dma = pltpu.SemaphoreType.DMA
    return pl.pallas_call(
        encode_kernel,
        out_shape=(
            jax.ShapeDtypeStruct((ROWS, HALF), bf16),
            jax.ShapeDtypeStruct((8, NPAD), jnp.int32),
        ),
        in_specs=[SMEM, VMEM, VMEM, ANY, ANY, ANY],
        out_specs=(ANY, VMEM),
        scratch_shapes=[
            pltpu.VMEM((ROWS, HALF), bf16),
            pltpu.VMEM((TOKENS, D), bf16),
            pltpu.VMEM((CHUNKS, D, CHUNK), bf16),
            pltpu.VMEM((CHUNKS, CHUNK, D), bf16),
            pltpu.VMEM((TOKENS, D), f32),
            pltpu.VMEM((BLOCK, CHUNK), f32),
            pltpu.VMEM((BLOCK, CHUNK), f32),
            pltpu.VMEM((8, NPAD), jnp.int32),
            pltpu.VMEM((ROWS, 2 * NPAD), bf16),
            pltpu.VMEM((NPAD, TOKENS), bf16),
            pltpu.VMEM((TOKENS, D), bf16),
            dma((BLOCKS,)),
            dma((CHUNKS,)),
            dma((CHUNKS,)),
            dma((PIECES,)),
        ],
        compiler_params=params(56),
        cost_estimate=cost(4 * TOKENS * D * FF, 20 * 2**20),
        name="encode",
    )(upper, owner, node_ids, states, expand_weight, contract_weight)


def fill_band(columns_ref, count_ref, values_ref, band, transposed):
    band[...] = jnp.zeros(band.shape, bf16)
    for r in range(2):
        for c in range(r, r + 3):
            tile = jnp.zeros((TILE, TILE), f32)
            for s in range(3):
                used = (s < count_ref[0, r]) & (columns_ref[0, r, s] == c)
                tile += jnp.where(used, 1.0, 0.0) * values_ref[0, r, s].astype(f32)
            rows, lanes = slice(r * TILE, (r + 1) * TILE), slice(c * TILE, (c + 1) * TILE)
            if transposed:
                band[lanes, rows] = tile.T.astype(bf16)
            else:
                band[rows, lanes] = tile.astype(bf16)


def spread_kernel(
    columns_ref, count_ref, values_ref, cotangent_ref, weight_ref, low_ref, high_ref, inner_hbm, band_t, inner, sem
):
    fill_band(columns_ref, count_ref, values_ref, band_t, True)
    grad_mix = dot_t(cotangent_ref[...], weight_ref[...]).astype(bf16)
    inner[...] = dot(band_t[TILE : TILE + SLOTS, :], grad_mix)
    copy = pltpu.make_async_copy(inner, inner_hbm, sem)
    copy.start()
    low_ref[...] = dot(band_t[:TILE, :], grad_mix).astype(bf16)
    high_ref[...] = dot(band_t[TILE + SLOTS :, :], grad_mix).astype(bf16)
    copy.wait()


def spread(columns, counts, values, cotangent, weight):
    return pl.pallas_call(
        spread_kernel,
        out_shape=(
            jax.ShapeDtypeStruct((TILE, D), bf16),
            jax.ShapeDtypeStruct((TILE, D), bf16),
            jax.ShapeDtypeStruct((SLOTS, D), f32),
        ),
        in_specs=[SMEM, SMEM, VMEM, VMEM, VMEM],
        out_specs=(VMEM, VMEM, ANY),
        scratch_shapes=[
            pltpu.VMEM((2 * SLOTS, SLOTS), bf16),
            pltpu.VMEM((SLOTS, D), f32),
            pltpu.SemaphoreType.DMA,
        ],
        compiler_params=params(63.9),
        cost_estimate=cost(10**9, 5 * 2**20),
        name="spread",
    )(columns, counts, values, cotangent, weight)


def prepare_kernel(
    columns_ref,
    count_ref,
    values_ref,
    order_ref,
    mix_hbm,
    mix_t_hbm,
    band_ref,
    band_t,
    mix,
    mix_t,
    sems,
):
    fill_band(columns_ref, count_ref, values_ref, band_ref, False)
    fill_band(columns_ref, count_ref, values_ref, band_t, True)

    def place(column):
        peer, slot = column >> 3, column & 3
        halo = jnp.where(peer < PEERS // 2, 2 * SLOTS - TILE, -PEERS) + 2 * peer + slot - 2
        return jnp.where(slot < 2, TILE + 2 * peer + slot, halo)

    shape = (2 * SLOTS, ROWS)
    moved = jnp.where(iota(shape, 0) == place(iota((1, ROWS), 1)), 1.0, 0.0)
    mix[...] = dot(band_ref[...], moved.astype(bf16)).astype(bf16)
    back = jnp.where(iota(shape[::-1], 1) == place(iota((ROWS, 1), 0)), 1.0, 0.0)
    mix_t[...] = dot(back.astype(bf16), band_t[...]).astype(bf16)
    copies = [
        pltpu.make_async_copy(mix, mix_hbm, sems.at[0]),
        pltpu.make_async_copy(mix_t, mix_t_hbm, sems.at[1]),
    ]
    for copy in copies:
        copy.start()
    for copy in copies:
        copy.wait()


def prepare(columns, counts, values, order):
    return pl.pallas_call(
        prepare_kernel,
        out_shape=(
            jax.ShapeDtypeStruct((SLOTS, ROWS), bf16),
            jax.ShapeDtypeStruct((ROWS, SLOTS), bf16),
            jax.ShapeDtypeStruct((SLOTS, 2 * SLOTS), bf16),
        ),
        in_specs=[SMEM, SMEM, VMEM, ANY],
        out_specs=(ANY, ANY, VMEM),
        scratch_shapes=[
            pltpu.VMEM((2 * SLOTS, SLOTS), bf16),
            pltpu.VMEM((SLOTS, ROWS), bf16),
            pltpu.VMEM((ROWS, SLOTS), bf16),
            pltpu.SemaphoreType.DMA((2,)),
        ],
        compiler_params=params(63.9),
        cost_estimate=cost(10**9, 4 * 2**20),
        name="prepare",
    )(columns, counts, values, order)


def middle_kernel(
    rows_hbm,
    mix_hbm,
    weight_hbm,
    inner_hbm,
    left_hbm,
    right_hbm,
    mix_t_hbm,
    top_hbm,
    bottom_hbm,
    out_hbm,
    acts,
    out,
    rows,
    mix,
    weight,
    inner,
    left,
    right,
    mix_t,
    back,
    sems,
    act_sems,
    out_sems,
):
    pairs = (
        (mix_hbm, mix),
        (rows_hbm, rows),
        (weight_hbm, weight),
        (inner_hbm, inner),
        (left_hbm, left),
        (right_hbm, right),
        (mix_t_hbm, mix_t),
    )
    copies = [pltpu.make_async_copy(a, b, sems.at[i]) for i, (a, b) in enumerate(pairs)]
    for copy in copies:
        copy.start()
    copies[0].wait()
    copies[1].wait()
    lane_half = ((iota((1, ROWS), 1) >> 2) & 1).astype(f32).astype(bf16)
    upper_mix = mix[...] * lane_half
    both = jnp.concatenate([mix[...] - upper_mix, upper_mix], axis=0)
    halves = dot(both, rows[...]).astype(bf16)
    mixed = jnp.concatenate([halves[:SLOTS], halves[SLOTS:]], axis=1)
    copies[2].wait()
    before = dot(mixed, weight[...])
    erf = 0.5 * (1.0 + lax.erf(before * ROOT_HALF))
    acted = (before * erf).astype(bf16)
    acts[...] = acted
    act_copies = [
        pltpu.make_async_copy(acts.at[pl.ds(i * TILE, TILE), :], to, act_sems.at[i])
        for i, to in enumerate((top_hbm, bottom_hbm))
    ]
    for copy in act_copies:
        copy.start()
    slope = erf + before * (INV_ROOT_TAU * jnp.exp(-0.5 * before * before))
    for copy in copies[3:6]:
        copy.wait()
    rims = jnp.concatenate([left[...], right[...]], axis=0).astype(f32)
    grad_before = ((inner[...] + rims) * slope).astype(bf16)
    grad_mix = dot_t(grad_before, weight[...]).astype(bf16)
    stacked = jnp.concatenate([grad_mix[:, :HALF], grad_mix[:, HALF:]], axis=0)
    copies[6].wait()
    row_half = ((iota((ROWS, 1), 0) >> 2) & 1).astype(f32).astype(bf16)
    upper_t = mix_t[...] * row_half
    both_t = jnp.concatenate([mix_t[...] - upper_t, upper_t], axis=1)
    back[...] = both_t
    send_rows(lambda r: dot(back[r, :], stacked), out, out_hbm, out_sems)
    for copy in act_copies:
        copy.wait()


def middle(*arrays):
    return pl.pallas_call(
        middle_kernel,
        out_shape=(
            jax.ShapeDtypeStruct((TILE, D), bf16),
            jax.ShapeDtypeStruct((TILE, D), bf16),
            jax.ShapeDtypeStruct((ROWS, HALF), bf16),
        ),
        in_specs=[ANY] * 7,
        out_specs=(ANY,) * 3,
        scratch_shapes=[pltpu.VMEM((SLOTS, D), bf16), pltpu.VMEM((ROWS, HALF), bf16)]
        + [pltpu.VMEM(a.shape, a.dtype) for a in arrays]
        + [pltpu.VMEM((ROWS, 2 * SLOTS), bf16)]
        + [pltpu.SemaphoreType.DMA((n,)) for n in (7, 2, PIECES)],
        compiler_params=params(63.9),
        cost_estimate=cost(3 * 10**9, 8 * 2**20),
        name="middle",
    )(*arrays)


def own_part_kernel(
    top_hbm, bottom_hbm, band_hbm, part_ref, first_ref, last_ref, acts, band, sems
):
    copies = [
        pltpu.make_async_copy(top_hbm, acts.at[pl.ds(0, TILE), :], sems.at[0]),
        pltpu.make_async_copy(bottom_hbm, acts.at[pl.ds(TILE, TILE), :], sems.at[1]),
        pltpu.make_async_copy(band_hbm, band, sems.at[2]),
    ]
    for copy in copies:
        copy.start()
    for copy in copies:
        copy.wait()
    part_ref[...] = dot(band[:, TILE : TILE + SLOTS], acts[...])
    first_ref[...] = band[:, :TILE]
    last_ref[...] = band[:, TILE + SLOTS :]


def own_part(*arrays):
    return pl.pallas_call(
        own_part_kernel,
        out_shape=(
            jax.ShapeDtypeStruct((SLOTS, D), f32),
            jax.ShapeDtypeStruct((SLOTS, TILE), bf16),
            jax.ShapeDtypeStruct((SLOTS, TILE), bf16),
        ),
        in_specs=[ANY] * 3,
        out_specs=(VMEM,) * 3,
        scratch_shapes=[
            pltpu.VMEM((SLOTS, D), bf16),
            pltpu.VMEM((SLOTS, 2 * SLOTS), bf16),
            pltpu.SemaphoreType.DMA((3,)),
        ],
        compiler_params=params(16),
        cost_estimate=cost(2 * 10**8, 3 * 2**20),
        name="own_part",
    )(*arrays)


def finish_kernel(part_ref, first_ref, last_ref, left_ref, right_ref, weight_ref, out_ref):
    mixed = part_ref[...] + dot(first_ref[...], left_ref[...]) + dot(last_ref[...], right_ref[...])
    out_ref[...] = dot(mixed.astype(bf16), weight_ref[...]).astype(bf16)


def finish(*arrays):
    return pl.pallas_call(
        finish_kernel,
        out_shape=jax.ShapeDtypeStruct((SLOTS, D), bf16),
        in_specs=[VMEM] * 6,
        out_specs=VMEM,
        compiler_params=params(16),
        cost_estimate=cost(10**9, 5 * 2**20),
        name="finish",
    )(*arrays)


def gather_kernel(target_ref, rows_ref, out_ref, pick):
    diagonal = iota((NODES, NPAD), 0) == iota((NODES, NPAD), 1)
    own_row = jnp.sum(jnp.where(diagonal, target_ref[0:1, :], 0), axis=1, keepdims=True)
    halo_row = jnp.sum(jnp.where(diagonal, target_ref[1:2, :], 0), axis=1, keepdims=True)
    lanes = iota((NODES, ROWS), 1)
    for u in range(2):
        hit = (lanes == own_row + 4 * u) | (lanes == halo_row + 4 * u)
        pick[u * NODES : (u + 1) * NODES, :] = jnp.where(hit, 1.0, 0.0).astype(bf16)
    picked = dot(pick[...], rows_ref[...]).astype(bf16)
    out_ref[:, :HALF] = picked[:NODES]
    out_ref[:, HALF:] = picked[NODES:]


def gather(target, rows):
    return pl.pallas_call(
        gather_kernel,
        out_shape=jax.ShapeDtypeStruct((NODES, D), bf16),
        in_specs=[VMEM, VMEM],
        out_specs=VMEM,
        scratch_shapes=[pltpu.VMEM((2 * NODES, ROWS), bf16)],
        compiler_params=params(16),
        cost_estimate=cost(4 * 10**8, 2 * 2**20),
        name="gather",
    )(target, rows)


def swap(rows):
    return lax.all_to_all(
        rows.reshape(PEERS, 8, HALF), ("enc", "dom"), split_axis=0, concat_axis=0, tiled=True
    ).reshape(ROWS, HALF)


def local(
    token_states,
    token_nodes,
    expand_weight,
    contract_weight,
    node_owner,
    tile_columns,
    tile_count,
    tile_values,
    first_weight,
    second_weight,
    output_cotangent,
):
    device = lax.axis_index("enc") * GROUP + lax.axis_index("dom")
    upper = (device >= PEERS // 2).astype(jnp.int32).reshape(1)
    rightward = [(i, i + 1) for i in range(GROUP - 1)]
    leftward = [(i + 1, i) for i in range(GROUP - 1)]
    outgoing, target = encode(
        upper, node_owner.reshape(1, NODES), token_nodes, token_states, expand_weight, contract_weight
    )
    arrived = swap(outgoing)
    target, later_cotangent = lax.optimization_barrier((target, output_cotangent))
    low, high, inner = spread(tile_columns, tile_count, tile_values, later_cotangent, second_weight)
    mix, mix_t, band = prepare(tile_columns, tile_count, tile_values, inner)
    from_right = lax.ppermute(low, "dom", leftward)
    from_left = lax.ppermute(high, "dom", rightward)
    top, bottom, grads = middle(arrived, mix, first_weight, inner, from_left, from_right, mix_t)
    returned = swap(grads)
    left = lax.ppermute(bottom, "dom", rightward)
    right = lax.ppermute(top, "dom", leftward)
    part, first, last = own_part(top, bottom, band)
    graph_output = finish(part, first, last, left, right, second_weight)
    return (graph_output, gather(target, returned))


def solution(mesh):
    rows = ("enc", "dom")
    placed = (
        P(rows, None),
        P(rows, None),
        P(),
        P(),
        P(rows, None),
        P(rows, None, None),
        P(rows, None),
        P(rows, None, None, None, None),
        P(),
        P(),
        P(rows, None),
    )
    return jax.shard_map(
        local,
        mesh=mesh,
        in_specs=placed,
        out_specs=(P(rows, None), P(rows, None)),
        check_vma=False,
    )
```

```python
import jax
import jax.numpy as jnp
from jax import lax
from jax.experimental import pallas as pl
from jax.experimental.pallas import tpu as pltpu
from jax.sharding import PartitionSpec as P

NODES = 192
NPAD = 256
TOKENS = 1024
D = 1024
FF = 4096
HALF = 512
PEERS = 128
GROUP = 8
ROWS = 1024
TILE = 128
SLOTS = 256

CHUNK = 512
CHUNKS = FF // CHUNK
BLOCK = 512
BLOCKS = TOKENS // BLOCK
AHEAD = 2
OPEN = (512, 512)
USUAL = (512, 512)
CLOSE = (256, 256, 256, 256)
PIECES = 4

bf16 = jnp.bfloat16
f32 = jnp.float32
EPS = 1e-07
ROOT_HALF = 0.7071067811865476
INV_ROOT_TAU = 0.3989422804014327

ANY = pl.BlockSpec(memory_space=pl.ANY)
VMEM = pl.BlockSpec(memory_space=pltpu.VMEM)
SMEM = pl.BlockSpec(memory_space=pltpu.SMEM)


def dot(a, b):
    return jnp.dot(a, b, preferred_element_type=f32)


def dot_t(a, b):
    return lax.dot_general(a, b, (((1,), (1,)), ((), ())), preferred_element_type=f32)


def iota(shape, dim):
    return lax.broadcasted_iota(jnp.int32, shape, dim)


def params(mib):
    return pltpu.CompilerParams(vmem_limit_bytes=int(mib * 2**20))


def cost(flops, moved):
    return pl.CostEstimate(flops=flops, bytes_accessed=moved, transcendentals=0)


def interleave(low, high):
    count = low.shape[0] // 8
    low, high = low.reshape(count, 8, HALF), high.reshape(count, 8, HALF)
    upper_rows = iota(low.shape, 1) >= 4
    even = jnp.where(upper_rows, pltpu.roll(high, 4, 1), low)
    odd = jnp.where(upper_rows, high, pltpu.roll(low, 4, 1))
    return jnp.stack([even, odd], axis=1).reshape(count * 16, HALF)


def send_rows(rows_of, out, out_hbm, sem):
    size = ROWS // PIECES
    copies = []
    for i in range(PIECES):
        rows = pl.ds(i * size, size)
        out[rows, :] = rows_of(pl.ds(i * size // 2, size // 2)).astype(bf16)
        copies.append(pltpu.make_async_copy(out.at[rows, :], out_hbm.at[rows, :], sem.at[i]))
        copies[-1].start()
    for copy in copies:
        copy.wait()


def encode_kernel(
    upper_ref,
    owner_ref,
    node_ref,
    states_hbm,
    expand_hbm,
    contract_hbm,
    out_hbm,
    target_ref,
    out,
    states,
    expand,
    contract,
    total,
    hidden_a,
    hidden_b,
    owner_pad,
    route,
    member,
    normed,
    state_sem,
    expand_sem,
    contract_sem,
    out_sem,
):
    def block_of(m):
        return pl.ds(m * BLOCK, BLOCK)

    def chunk_of(c):
        return pl.ds(pl.multiple_of(c * CHUNK, CHUNK), CHUNK)

    def start_expand(c):
        pltpu.make_async_copy(
            expand_hbm.at[:, chunk_of(c)], expand.at[c], expand_sem.at[c]
        ).start()

    def start(c):
        if not isinstance(c, int) or c > 0:
            start_expand(c)
        pltpu.make_async_copy(
            contract_hbm.at[chunk_of(c), :], contract.at[c], contract_sem.at[c]
        ).start()

    def wait_expand(c):
        pltpu.make_async_copy(
            expand_hbm.at[:, chunk_of(c)], expand.at[c], expand_sem.at[c]
        ).wait()

    def wait(c):
        if not isinstance(c, int) or c > 0:
            wait_expand(c)
        pltpu.make_async_copy(
            contract_hbm.at[chunk_of(c), :], contract.at[c], contract_sem.at[c]
        ).wait()

    def state_copy(m):
        return pltpu.make_async_copy(
            states_hbm.at[block_of(m), :], states.at[block_of(m), :], state_sem.at[m]
        )

    state_copy(0).start()
    start_expand(0)
    for m in range(1, BLOCKS):
        state_copy(m).start()
    start(0)

    owner_pad[...] = jnp.full((8, NPAD), -4096, jnp.int32)
    owner_pad[0:1, 0:NODES] = owner_ref[...]
    owner = owner_pad[0:1, :]
    named = jnp.where(iota((PEERS, NPAD), 0) == owner, 1.0, 0.0).astype(bf16)
    before = jnp.where(iota((NPAD, NPAD), 0) < iota((NPAD, NPAD), 1), 1.0, 0.0).astype(bf16)
    earlier = dot(named, before)
    rank = jnp.sum(named.astype(f32) * earlier, axis=0, keepdims=True).astype(jnp.int32)
    own_row = owner * 8 + rank
    upper = upper_ref[0]
    beside = owner + jnp.where(upper == 1, 1, -1)
    edge = jnp.where(upper == 1, GROUP - 1, 0)
    has_beside = (owner & (GROUP - 1)) != edge
    halo_row = jnp.where(has_beside, beside * 8 + 2 + rank, -4096)
    target_ref[...] = jnp.where(iota((8, NPAD), 0) == 0, own_row, halo_row)
    rows = iota((ROWS // 2, NPAD), 0)
    hit = (rows == owner * 4 + rank) | (rows == jnp.where(has_beside, beside * 4 + 2 + rank, -4096))
    route[...] = jnp.where(hit, 1.0, 0.0).astype(bf16)
    mask = jnp.where(iota((NPAD, TOKENS), 0) == node_ref[...], 1.0, 0.0)
    member[...] = mask.astype(bf16)
    counts = jnp.maximum(jnp.sum(mask, axis=1, keepdims=True), 1.0)

    def first(c, r, n):
        return dot(states[pl.ds(r, n), :], expand[c])

    def second(c, r, n, values, opening):
        acted = 0.5 * values * (1.0 + lax.erf(values * ROOT_HALF))
        product = dot(acted.astype(bf16), contract[c])
        rows = pl.ds(r, n)
        total[rows, :] = product if opening else total[rows, :] + product

    buffers = (hidden_a, hidden_b)

    def step(c, sizes, following, opening=False, closing=False):
        starts = [sum(sizes[:k]) for k in range(len(sizes))]
        for k, (r, n) in enumerate(zip(starts, sizes)):
            now, later = buffers[k % 2], buffers[(k + 1) % 2]
            if k + 1 < len(sizes):
                later[: sizes[k + 1], :] = first(c, starts[k + 1], sizes[k + 1])
            elif not closing:
                if opening:
                    start(2)
                    wait(1)
                later[:following, :] = first(c + 1, 0, following)
            second(c, r, n, now[:n, :], opening)
            if closing:
                settle(pl.ds(r, n))

    def settle(rows):
        mixed = total[rows, :] + states[rows, :].astype(f32)
        centred = mixed - jnp.mean(mixed, axis=1, keepdims=True)
        variance = jnp.mean(centred * centred, axis=1, keepdims=True)
        normed[rows, :] = (centred * lax.rsqrt(variance + EPS)).astype(bf16)

    state_copy(0).wait()
    wait_expand(0)
    start(1)
    hidden_a[:OPEN[0], :] = first(0, 0, OPEN[0])
    for m in range(1, BLOCKS):
        state_copy(m).wait()
    wait(0)
    step(0, OPEN, USUAL[0], opening=True)

    def middle_step(c, carry):
        @pl.when(c + AHEAD < CHUNKS)
        def _():
            start(c + AHEAD)

        wait(c + 1)
        step(c, USUAL, USUAL[0])
        return carry

    lax.fori_loop(1, CHUNKS - 2, middle_step, 0)
    wait(CHUNKS - 1)
    step(CHUNKS - 2, USUAL, CLOSE[0])
    step(CHUNKS - 1, CLOSE, None, closing=True)
    summed = dot(member[...], normed[...])
    embeds = (summed / counts).astype(bf16)
    send_rows(
        lambda r: interleave(dot(route[r, :], embeds[:, :HALF]), dot(route[r, :], embeds[:, HALF:])),
        out,
        out_hbm,
        out_sem,
    )


def encode(upper, owner, node_ids, states, expand_weight, contract_weight):
    dma = pltpu.SemaphoreType.DMA
    return pl.pallas_call(
        encode_kernel,
        out_shape=(
            jax.ShapeDtypeStruct((ROWS, HALF), bf16),
            jax.ShapeDtypeStruct((8, NPAD), jnp.int32),
        ),
        in_specs=[SMEM, VMEM, VMEM, ANY, ANY, ANY],
        out_specs=(ANY, VMEM),
        scratch_shapes=[
            pltpu.VMEM((ROWS, HALF), bf16),
            pltpu.VMEM((TOKENS, D), bf16),
            pltpu.VMEM((CHUNKS, D, CHUNK), bf16),
            pltpu.VMEM((CHUNKS, CHUNK, D), bf16),
            pltpu.VMEM((TOKENS, D), f32),
            pltpu.VMEM((BLOCK, CHUNK), f32),
            pltpu.VMEM((BLOCK, CHUNK), f32),
            pltpu.VMEM((8, NPAD), jnp.int32),
            pltpu.VMEM((ROWS // 2, NPAD), bf16),
            pltpu.VMEM((NPAD, TOKENS), bf16),
            pltpu.VMEM((TOKENS, D), bf16),
            dma((BLOCKS,)),
            dma((CHUNKS,)),
            dma((CHUNKS,)),
            dma((PIECES,)),
        ],
        compiler_params=params(56),
        cost_estimate=cost(4 * TOKENS * D * FF, 20 * 2**20),
        name="encode",
    )(upper, owner, node_ids, states, expand_weight, contract_weight)


def fill_band(columns_ref, count_ref, values_ref, band, transposed):
    band[...] = jnp.zeros(band.shape, bf16)
    for r in range(2):
        for c in range(r, r + 3):
            tile = jnp.zeros((TILE, TILE), f32)
            for s in range(3):
                used = (s < count_ref[0, r]) & (columns_ref[0, r, s] == c)
                tile += jnp.where(used, 1.0, 0.0) * values_ref[0, r, s].astype(f32)
            rows, lanes = slice(r * TILE, (r + 1) * TILE), slice(c * TILE, (c + 1) * TILE)
            if transposed:
                band[lanes, rows] = tile.T.astype(bf16)
            else:
                band[rows, lanes] = tile.astype(bf16)


def spread_kernel(
    columns_ref, count_ref, values_ref, cotangent_ref, weight_ref, low_ref, high_ref, inner_hbm, band_t, inner, sem
):
    fill_band(columns_ref, count_ref, values_ref, band_t, True)
    grad_mix = dot_t(cotangent_ref[...], weight_ref[...]).astype(bf16)
    inner[...] = dot(band_t[TILE : TILE + SLOTS, :], grad_mix)
    copy = pltpu.make_async_copy(inner, inner_hbm, sem)
    copy.start()
    low_ref[...] = dot(band_t[:TILE, :], grad_mix).astype(bf16)
    high_ref[...] = dot(band_t[TILE + SLOTS :, :], grad_mix).astype(bf16)
    copy.wait()


def spread(columns, counts, values, cotangent, weight):
    return pl.pallas_call(
        spread_kernel,
        out_shape=(
            jax.ShapeDtypeStruct((TILE, D), bf16),
            jax.ShapeDtypeStruct((TILE, D), bf16),
            jax.ShapeDtypeStruct((SLOTS, D), f32),
        ),
        in_specs=[SMEM, SMEM, VMEM, VMEM, VMEM],
        out_specs=(VMEM, VMEM, ANY),
        scratch_shapes=[
            pltpu.VMEM((2 * SLOTS, SLOTS), bf16),
            pltpu.VMEM((SLOTS, D), f32),
            pltpu.SemaphoreType.DMA,
        ],
        compiler_params=params(63.9),
        cost_estimate=cost(10**9, 5 * 2**20),
        name="spread",
    )(columns, counts, values, cotangent, weight)


def prepare_kernel(
    columns_ref,
    count_ref,
    values_ref,
    order_ref,
    mix_hbm,
    mix_t_hbm,
    band_ref,
    band_t,
    mix,
    mix_t,
    sems,
):
    fill_band(columns_ref, count_ref, values_ref, band_ref, False)
    fill_band(columns_ref, count_ref, values_ref, band_t, True)

    def place(column):
        peer, slot = column >> 3, column & 3
        halo = jnp.where(peer < PEERS // 2, 2 * SLOTS - TILE, -PEERS) + 2 * peer + slot - 2
        return jnp.where(slot < 2, TILE + 2 * peer + slot, halo)

    shape = (2 * SLOTS, ROWS)
    moved = jnp.where(iota(shape, 0) == place(iota((1, ROWS), 1)), 1.0, 0.0)
    mix[...] = dot(band_ref[...], moved.astype(bf16)).astype(bf16)
    pair = iota((ROWS // 2, 1), 0)
    source = place((pair >> 2) * 8 + (pair & 3))
    back = jnp.where(iota((ROWS // 2, 2 * SLOTS), 1) == source, 1.0, 0.0)
    mix_t[...] = dot(back.astype(bf16), band_t[...]).astype(bf16)
    copies = [
        pltpu.make_async_copy(mix, mix_hbm, sems.at[0]),
        pltpu.make_async_copy(mix_t, mix_t_hbm, sems.at[1]),
    ]
    for copy in copies:
        copy.start()
    for copy in copies:
        copy.wait()


def prepare(columns, counts, values, order):
    return pl.pallas_call(
        prepare_kernel,
        out_shape=(
            jax.ShapeDtypeStruct((SLOTS, ROWS), bf16),
            jax.ShapeDtypeStruct((ROWS // 2, SLOTS), bf16),
            jax.ShapeDtypeStruct((SLOTS, 2 * SLOTS), bf16),
        ),
        in_specs=[SMEM, SMEM, VMEM, ANY],
        out_specs=(ANY, ANY, VMEM),
        scratch_shapes=[
            pltpu.VMEM((2 * SLOTS, SLOTS), bf16),
            pltpu.VMEM((SLOTS, ROWS), bf16),
            pltpu.VMEM((ROWS // 2, SLOTS), bf16),
            pltpu.SemaphoreType.DMA((2,)),
        ],
        compiler_params=params(63.9),
        cost_estimate=cost(10**9, 4 * 2**20),
        name="prepare",
    )(columns, counts, values, order)


def middle_kernel(
    rows_hbm,
    mix_hbm,
    weight_hbm,
    inner_hbm,
    left_hbm,
    right_hbm,
    mix_t_hbm,
    top_hbm,
    bottom_hbm,
    out_hbm,
    acts,
    out,
    rows,
    mix,
    weight,
    inner,
    left,
    right,
    mix_t,
    sems,
    act_sems,
    out_sems,
):
    pairs = (
        (mix_hbm, mix),
        (rows_hbm, rows),
        (weight_hbm, weight),
        (inner_hbm, inner),
        (left_hbm, left),
        (right_hbm, right),
        (mix_t_hbm, mix_t),
    )
    copies = [pltpu.make_async_copy(a, b, sems.at[i]) for i, (a, b) in enumerate(pairs)]
    for copy in copies:
        copy.start()
    copies[0].wait()
    copies[1].wait()
    lane_half = ((iota((1, ROWS), 1) >> 2) & 1).astype(f32).astype(bf16)
    upper_mix = mix[...] * lane_half
    both = jnp.concatenate([mix[...] - upper_mix, upper_mix], axis=0)
    halves = dot(both, rows[...]).astype(bf16)
    mixed = jnp.concatenate([halves[:SLOTS], halves[SLOTS:]], axis=1)
    copies[2].wait()
    before = dot(mixed, weight[...])
    erf = 0.5 * (1.0 + lax.erf(before * ROOT_HALF))
    acted = (before * erf).astype(bf16)
    acts[...] = acted
    act_copies = [
        pltpu.make_async_copy(acts.at[pl.ds(i * TILE, TILE), :], to, act_sems.at[i])
        for i, to in enumerate((top_hbm, bottom_hbm))
    ]
    for copy in act_copies:
        copy.start()
    slope = erf + before * (INV_ROOT_TAU * jnp.exp(-0.5 * before * before))
    for copy in copies[3:6]:
        copy.wait()
    rims = jnp.concatenate([left[...], right[...]], axis=0).astype(f32)
    grad_before = ((inner[...] + rims) * slope).astype(bf16)
    grad_mix = dot_t(grad_before, weight[...]).astype(bf16)
    copies[6].wait()
    send_rows(
        lambda r: interleave(dot(mix_t[r, :], grad_mix[:, :HALF]), dot(mix_t[r, :], grad_mix[:, HALF:])),
        out,
        out_hbm,
        out_sems,
    )
    for copy in act_copies:
        copy.wait()


def middle(*arrays):
    return pl.pallas_call(
        middle_kernel,
        out_shape=(
            jax.ShapeDtypeStruct((TILE, D), bf16),
            jax.ShapeDtypeStruct((TILE, D), bf16),
            jax.ShapeDtypeStruct((ROWS, HALF), bf16),
        ),
        in_specs=[ANY] * 7,
        out_specs=(ANY,) * 3,
        scratch_shapes=[pltpu.VMEM((SLOTS, D), bf16), pltpu.VMEM((ROWS, HALF), bf16)]
        + [pltpu.VMEM(a.shape, a.dtype) for a in arrays]
        + [pltpu.SemaphoreType.DMA((n,)) for n in (7, 2, PIECES)],
        compiler_params=params(63.9),
        cost_estimate=cost(3 * 10**9, 8 * 2**20),
        name="middle",
    )(*arrays)


def own_part_kernel(
    top_hbm, bottom_hbm, band_hbm, part_ref, first_ref, last_ref, acts, band, sems
):
    copies = [
        pltpu.make_async_copy(top_hbm, acts.at[pl.ds(0, TILE), :], sems.at[0]),
        pltpu.make_async_copy(bottom_hbm, acts.at[pl.ds(TILE, TILE), :], sems.at[1]),
        pltpu.make_async_copy(band_hbm, band, sems.at[2]),
    ]
    for copy in copies:
        copy.start()
    for copy in copies:
        copy.wait()
    part_ref[...] = dot(band[:, TILE : TILE + SLOTS], acts[...])
    first_ref[...] = band[:, :TILE]
    last_ref[...] = band[:, TILE + SLOTS :]


def own_part(*arrays):
    return pl.pallas_call(
        own_part_kernel,
        out_shape=(
            jax.ShapeDtypeStruct((SLOTS, D), f32),
            jax.ShapeDtypeStruct((SLOTS, TILE), bf16),
            jax.ShapeDtypeStruct((SLOTS, TILE), bf16),
        ),
        in_specs=[ANY] * 3,
        out_specs=(VMEM,) * 3,
        scratch_shapes=[
            pltpu.VMEM((SLOTS, D), bf16),
            pltpu.VMEM((SLOTS, 2 * SLOTS), bf16),
            pltpu.SemaphoreType.DMA((3,)),
        ],
        compiler_params=params(16),
        cost_estimate=cost(2 * 10**8, 3 * 2**20),
        name="own_part",
    )(*arrays)


def finish_kernel(part_ref, first_ref, last_ref, left_ref, right_ref, weight_ref, out_ref):
    mixed = part_ref[...] + dot(first_ref[...], left_ref[...]) + dot(last_ref[...], right_ref[...])
    out_ref[...] = dot(mixed.astype(bf16), weight_ref[...]).astype(bf16)


def finish(*arrays):
    return pl.pallas_call(
        finish_kernel,
        out_shape=jax.ShapeDtypeStruct((SLOTS, D), bf16),
        in_specs=[VMEM] * 6,
        out_specs=VMEM,
        compiler_params=params(16),
        cost_estimate=cost(10**9, 5 * 2**20),
        name="finish",
    )(*arrays)


def gather_kernel(target_ref, rows_ref, out_ref, pick):
    diagonal = iota((NODES, NPAD), 0) == iota((NODES, NPAD), 1)
    own_row = jnp.sum(jnp.where(diagonal, target_ref[0:1, :], 0), axis=1, keepdims=True)
    halo_row = jnp.sum(jnp.where(diagonal, target_ref[1:2, :], 0), axis=1, keepdims=True)
    lanes = iota((NODES, ROWS), 1)
    for u in range(2):
        hit = (lanes == own_row + 4 * u) | (lanes == halo_row + 4 * u)
        pick[u * NODES : (u + 1) * NODES, :] = jnp.where(hit, 1.0, 0.0).astype(bf16)
    picked = dot(pick[...], rows_ref[...]).astype(bf16)
    out_ref[:, :HALF] = picked[:NODES]
    out_ref[:, HALF:] = picked[NODES:]


def gather(target, rows):
    return pl.pallas_call(
        gather_kernel,
        out_shape=jax.ShapeDtypeStruct((NODES, D), bf16),
        in_specs=[VMEM, VMEM],
        out_specs=VMEM,
        scratch_shapes=[pltpu.VMEM((2 * NODES, ROWS), bf16)],
        compiler_params=params(16),
        cost_estimate=cost(4 * 10**8, 2 * 2**20),
        name="gather",
    )(target, rows)


def swap(rows):
    return lax.all_to_all(
        rows.reshape(PEERS, 8, HALF), ("enc", "dom"), split_axis=0, concat_axis=0, tiled=True
    ).reshape(ROWS, HALF)


def local(
    token_states,
    token_nodes,
    expand_weight,
    contract_weight,
    node_owner,
    tile_columns,
    tile_count,
    tile_values,
    first_weight,
    second_weight,
    output_cotangent,
):
    device = lax.axis_index("enc") * GROUP + lax.axis_index("dom")
    upper = (device >= PEERS // 2).astype(jnp.int32).reshape(1)
    rightward = [(i, i + 1) for i in range(GROUP - 1)]
    leftward = [(i + 1, i) for i in range(GROUP - 1)]
    outgoing, target = encode(
        upper, node_owner.reshape(1, NODES), token_nodes, token_states, expand_weight, contract_weight
    )
    arrived = swap(outgoing)
    target, later_cotangent = lax.optimization_barrier((target, output_cotangent))
    low, high, inner = spread(tile_columns, tile_count, tile_values, later_cotangent, second_weight)
    mix, mix_t, band = prepare(tile_columns, tile_count, tile_values, inner)
    from_right = lax.ppermute(low, "dom", leftward)
    from_left = lax.ppermute(high, "dom", rightward)
    top, bottom, grads = middle(arrived, mix, first_weight, inner, from_left, from_right, mix_t)
    returned = swap(grads)
    left = lax.ppermute(bottom, "dom", rightward)
    right = lax.ppermute(top, "dom", leftward)
    part, first, last = own_part(top, bottom, band)
    graph_output = finish(part, first, last, left, right, second_weight)
    return (graph_output, gather(target, returned))


def solution(mesh):
    rows = ("enc", "dom")
    placed = (
        P(rows, None),
        P(rows, None),
        P(),
        P(),
        P(rows, None),
        P(rows, None, None),
        P(rows, None),
        P(rows, None, None, None, None),
        P(),
        P(),
        P(rows, None),
    )
    return jax.shard_map(
        local,
        mesh=mesh,
        in_specs=placed,
        out_specs=(P(rows, None), P(rows, None)),
        check_vma=False,
    )
```

```python
import jax
import jax.numpy as jnp
from jax import lax
from jax.experimental import pallas as pl
from jax.experimental.pallas import tpu as pltpu
from jax.sharding import PartitionSpec as P

NODES = 192
NPAD = 256
TOKENS = 1024
D = 1024
FF = 4096
HALF = 512
PEERS = 128
GROUP = 8
ROWS = 1024
TILE = 128
SLOTS = 256

CHUNK = 512
CHUNKS = FF // CHUNK
BLOCK = 512
BLOCKS = TOKENS // BLOCK
AHEAD = 2
OPEN = (512, 512)
USUAL = (512, 512)
CLOSE = (256, 256, 256, 256)
PIECES = 2

bf16 = jnp.bfloat16
f32 = jnp.float32
EPS = 1e-07
ROOT_HALF = 0.7071067811865476
INV_ROOT_TAU = 0.3989422804014327

ANY = pl.BlockSpec(memory_space=pl.ANY)
VMEM = pl.BlockSpec(memory_space=pltpu.VMEM)
SMEM = pl.BlockSpec(memory_space=pltpu.SMEM)


def dot(a, b):
    return jnp.dot(a, b, preferred_element_type=f32)


def dot_t(a, b):
    return lax.dot_general(a, b, (((1,), (1,)), ((), ())), preferred_element_type=f32)


def iota(shape, dim):
    return lax.broadcasted_iota(jnp.int32, shape, dim)


def params(mib):
    return pltpu.CompilerParams(vmem_limit_bytes=int(mib * 2**20))


def cost(flops, moved):
    return pl.CostEstimate(flops=flops, bytes_accessed=moved, transcendentals=0)


def interleave(low, high):
    count = low.shape[0] // 8
    low, high = low.reshape(count, 8, HALF), high.reshape(count, 8, HALF)
    upper_rows = iota(low.shape, 1) >= 4
    even = jnp.where(upper_rows, pltpu.roll(high, 4, 1), low)
    odd = jnp.where(upper_rows, high, pltpu.roll(low, 4, 1))
    return jnp.stack([even, odd], axis=1).reshape(count * 16, HALF)


def send_rows(rows_of, out, out_hbm, sem):
    size = ROWS // PIECES
    copies = []
    for i in range(PIECES):
        rows = pl.ds(i * size, size)
        out[rows, :] = rows_of(pl.ds(i * size // 2, size // 2)).astype(bf16)
        copies.append(pltpu.make_async_copy(out.at[rows, :], out_hbm.at[rows, :], sem.at[i]))
        copies[-1].start()
    for copy in copies:
        copy.wait()


def encode_kernel(
    upper_ref,
    owner_ref,
    node_ref,
    states_hbm,
    expand_hbm,
    contract_hbm,
    out_hbm,
    target_ref,
    out,
    states,
    expand,
    contract,
    total,
    hidden_a,
    hidden_b,
    owner_pad,
    route,
    member,
    normed,
    state_sem,
    expand_sem,
    contract_sem,
    out_sem,
):
    def block_of(m):
        return pl.ds(m * BLOCK, BLOCK)

    def chunk_of(c):
        return pl.ds(pl.multiple_of(c * CHUNK, CHUNK), CHUNK)

    def start_expand(c):
        pltpu.make_async_copy(
            expand_hbm.at[:, chunk_of(c)], expand.at[c], expand_sem.at[c]
        ).start()

    def start(c):
        if not isinstance(c, int) or c > 0:
            start_expand(c)
        pltpu.make_async_copy(
            contract_hbm.at[chunk_of(c), :], contract.at[c], contract_sem.at[c]
        ).start()

    def wait_expand(c):
        pltpu.make_async_copy(
            expand_hbm.at[:, chunk_of(c)], expand.at[c], expand_sem.at[c]
        ).wait()

    def wait(c):
        if not isinstance(c, int) or c > 0:
            wait_expand(c)
        pltpu.make_async_copy(
            contract_hbm.at[chunk_of(c), :], contract.at[c], contract_sem.at[c]
        ).wait()

    def state_copy(m):
        return pltpu.make_async_copy(
            states_hbm.at[block_of(m), :], states.at[block_of(m), :], state_sem.at[m]
        )

    state_copy(0).start()
    start_expand(0)
    for m in range(1, BLOCKS):
        state_copy(m).start()
    start(0)

    owner_pad[...] = jnp.full((8, NPAD), -4096, jnp.int32)
    owner_pad[0:1, 0:NODES] = owner_ref[...]
    owner = owner_pad[0:1, :]
    named = jnp.where(iota((PEERS, NPAD), 0) == owner, 1.0, 0.0).astype(bf16)
    before = jnp.where(iota((NPAD, NPAD), 0) < iota((NPAD, NPAD), 1), 1.0, 0.0).astype(bf16)
    earlier = dot(named, before)
    rank = jnp.sum(named.astype(f32) * earlier, axis=0, keepdims=True).astype(jnp.int32)
    own_row = owner * 8 + rank
    upper = upper_ref[0]
    beside = owner + jnp.where(upper == 1, 1, -1)
    edge = jnp.where(upper == 1, GROUP - 1, 0)
    has_beside = (owner & (GROUP - 1)) != edge
    halo_row = jnp.where(has_beside, beside * 8 + 2 + rank, -4096)
    target_ref[...] = jnp.where(iota((8, NPAD), 0) == 0, own_row, halo_row)
    rows = iota((ROWS // 2, NPAD), 0)
    hit = (rows == owner * 4 + rank) | (rows == jnp.where(has_beside, beside * 4 + 2 + rank, -4096))
    route[...] = jnp.where(hit, 1.0, 0.0).astype(bf16)
    mask = jnp.where(iota((NPAD, TOKENS), 0) == node_ref[...], 1.0, 0.0)
    member[...] = mask.astype(bf16)
    counts = jnp.maximum(jnp.sum(mask, axis=1, keepdims=True), 1.0)

    def first(c, r, n):
        return dot(states[pl.ds(r, n), :], expand[c])

    def second(c, r, n, values, opening):
        acted = 0.5 * values * (1.0 + lax.erf(values * ROOT_HALF))
        product = dot(acted.astype(bf16), contract[c])
        rows = pl.ds(r, n)
        total[rows, :] = product if opening else total[rows, :] + product

    buffers = (hidden_a, hidden_b)

    def step(c, sizes, following, opening=False, closing=False):
        starts = [sum(sizes[:k]) for k in range(len(sizes))]
        for k, (r, n) in enumerate(zip(starts, sizes)):
            now, later = buffers[k % 2], buffers[(k + 1) % 2]
            if k + 1 < len(sizes):
                later[: sizes[k + 1], :] = first(c, starts[k + 1], sizes[k + 1])
            elif not closing:
                if opening:
                    start(2)
                    wait(1)
                later[:following, :] = first(c + 1, 0, following)
            second(c, r, n, now[:n, :], opening)
            if closing:
                settle(pl.ds(r, n))

    def settle(rows):
        mixed = total[rows, :] + states[rows, :].astype(f32)
        centred = mixed - jnp.mean(mixed, axis=1, keepdims=True)
        variance = jnp.mean(centred * centred, axis=1, keepdims=True)
        normed[rows, :] = (centred * lax.rsqrt(variance + EPS)).astype(bf16)

    state_copy(0).wait()
    wait_expand(0)
    start(1)
    hidden_a[:OPEN[0], :] = first(0, 0, OPEN[0])
    for m in range(1, BLOCKS):
        state_copy(m).wait()
    wait(0)
    step(0, OPEN, USUAL[0], opening=True)

    def middle_step(c, carry):
        @pl.when(c + AHEAD < CHUNKS)
        def _():
            start(c + AHEAD)

        wait(c + 1)
        step(c, USUAL, USUAL[0])
        return carry

    lax.fori_loop(1, CHUNKS - 2, middle_step, 0)
    wait(CHUNKS - 1)
    step(CHUNKS - 2, USUAL, CLOSE[0])
    step(CHUNKS - 1, CLOSE, None, closing=True)
    summed = dot(member[...], normed[...])
    embeds = (summed / counts).astype(bf16)
    send_rows(
        lambda r: interleave(dot(route[r, :], embeds[:, :HALF]), dot(route[r, :], embeds[:, HALF:])),
        out,
        out_hbm,
        out_sem,
    )


def encode(upper, owner, node_ids, states, expand_weight, contract_weight):
    dma = pltpu.SemaphoreType.DMA
    return pl.pallas_call(
        encode_kernel,
        out_shape=(
            jax.ShapeDtypeStruct((ROWS, HALF), bf16),
            jax.ShapeDtypeStruct((8, NPAD), jnp.int32),
        ),
        in_specs=[SMEM, VMEM, VMEM, ANY, ANY, ANY],
        out_specs=(ANY, VMEM),
        scratch_shapes=[
            pltpu.VMEM((ROWS, HALF), bf16),
            pltpu.VMEM((TOKENS, D), bf16),
            pltpu.VMEM((CHUNKS, D, CHUNK), bf16),
            pltpu.VMEM((CHUNKS, CHUNK, D), bf16),
            pltpu.VMEM((TOKENS, D), f32),
            pltpu.VMEM((BLOCK, CHUNK), f32),
            pltpu.VMEM((BLOCK, CHUNK), f32),
            pltpu.VMEM((8, NPAD), jnp.int32),
            pltpu.VMEM((ROWS // 2, NPAD), bf16),
            pltpu.VMEM((NPAD, TOKENS), bf16),
            pltpu.VMEM((TOKENS, D), bf16),
            dma((BLOCKS,)),
            dma((CHUNKS,)),
            dma((CHUNKS,)),
            dma((PIECES,)),
        ],
        compiler_params=params(56),
        cost_estimate=cost(4 * TOKENS * D * FF, 20 * 2**20),
        name="encode",
    )(upper, owner, node_ids, states, expand_weight, contract_weight)


def fill_band(columns_ref, count_ref, values_ref, band, transposed):
    band[...] = jnp.zeros(band.shape, bf16)
    for r in range(2):
        for c in range(r, r + 3):
            tile = jnp.zeros((TILE, TILE), f32)
            for s in range(3):
                used = (s < count_ref[0, r]) & (columns_ref[0, r, s] == c)
                tile += jnp.where(used, 1.0, 0.0) * values_ref[0, r, s].astype(f32)
            rows, lanes = slice(r * TILE, (r + 1) * TILE), slice(c * TILE, (c + 1) * TILE)
            if transposed:
                band[lanes, rows] = tile.T.astype(bf16)
            else:
                band[rows, lanes] = tile.astype(bf16)


def spread_kernel(
    columns_ref, count_ref, values_ref, cotangent_ref, weight_ref, low_ref, high_ref, inner_hbm, band_t, inner, sem
):
    fill_band(columns_ref, count_ref, values_ref, band_t, True)
    grad_mix = dot_t(cotangent_ref[...], weight_ref[...]).astype(bf16)
    inner[...] = dot(band_t[TILE : TILE + SLOTS, :], grad_mix)
    copy = pltpu.make_async_copy(inner, inner_hbm, sem)
    copy.start()
    low_ref[...] = dot(band_t[:TILE, :], grad_mix).astype(bf16)
    high_ref[...] = dot(band_t[TILE + SLOTS :, :], grad_mix).astype(bf16)
    copy.wait()


def spread(columns, counts, values, cotangent, weight):
    return pl.pallas_call(
        spread_kernel,
        out_shape=(
            jax.ShapeDtypeStruct((TILE, D), bf16),
            jax.ShapeDtypeStruct((TILE, D), bf16),
            jax.ShapeDtypeStruct((SLOTS, D), f32),
        ),
        in_specs=[SMEM, SMEM, VMEM, VMEM, VMEM],
        out_specs=(VMEM, VMEM, ANY),
        scratch_shapes=[
            pltpu.VMEM((2 * SLOTS, SLOTS), bf16),
            pltpu.VMEM((SLOTS, D), f32),
            pltpu.SemaphoreType.DMA,
        ],
        compiler_params=params(63.9),
        cost_estimate=cost(10**9, 5 * 2**20),
        name="spread",
    )(columns, counts, values, cotangent, weight)


def prepare_kernel(
    columns_ref,
    count_ref,
    values_ref,
    order_ref,
    mix_hbm,
    mix_t_hbm,
    band_ref,
    band_t,
    mix,
    mix_t,
    sems,
):
    fill_band(columns_ref, count_ref, values_ref, band_ref, False)
    fill_band(columns_ref, count_ref, values_ref, band_t, True)

    def place(column):
        peer, slot = column >> 3, column & 3
        halo = jnp.where(peer < PEERS // 2, 2 * SLOTS - TILE, -PEERS) + 2 * peer + slot - 2
        return jnp.where(slot < 2, TILE + 2 * peer + slot, halo)

    shape = (2 * SLOTS, ROWS)
    moved = jnp.where(iota(shape, 0) == place(iota((1, ROWS), 1)), 1.0, 0.0)
    mix[...] = dot(band_ref[...], moved.astype(bf16)).astype(bf16)
    pair = iota((ROWS // 2, 1), 0)
    source = place((pair >> 2) * 8 + (pair & 3))
    back = jnp.where(iota((ROWS // 2, 2 * SLOTS), 1) == source, 1.0, 0.0)
    mix_t[...] = dot(back.astype(bf16), band_t[...]).astype(bf16)
    copies = [
        pltpu.make_async_copy(mix, mix_hbm, sems.at[0]),
        pltpu.make_async_copy(mix_t, mix_t_hbm, sems.at[1]),
    ]
    for copy in copies:
        copy.start()
    for copy in copies:
        copy.wait()


def prepare(columns, counts, values, order):
    return pl.pallas_call(
        prepare_kernel,
        out_shape=(
            jax.ShapeDtypeStruct((SLOTS, ROWS), bf16),
            jax.ShapeDtypeStruct((ROWS // 2, SLOTS), bf16),
            jax.ShapeDtypeStruct((SLOTS, 2 * SLOTS), bf16),
        ),
        in_specs=[SMEM, SMEM, VMEM, ANY],
        out_specs=(ANY, ANY, VMEM),
        scratch_shapes=[
            pltpu.VMEM((2 * SLOTS, SLOTS), bf16),
            pltpu.VMEM((SLOTS, ROWS), bf16),
            pltpu.VMEM((ROWS // 2, SLOTS), bf16),
            pltpu.SemaphoreType.DMA((2,)),
        ],
        compiler_params=params(63.9),
        cost_estimate=cost(10**9, 4 * 2**20),
        name="prepare",
    )(columns, counts, values, order)


def middle_kernel(
    rows_hbm,
    mix_hbm,
    weight_hbm,
    inner_hbm,
    left_hbm,
    right_hbm,
    mix_t_hbm,
    top_hbm,
    bottom_hbm,
    out_hbm,
    acts,
    out,
    rows,
    mix,
    weight,
    inner,
    left,
    right,
    mix_t,
    sems,
    act_sems,
    out_sems,
):
    pairs = (
        (mix_hbm, mix),
        (rows_hbm, rows),
        (weight_hbm, weight),
        (inner_hbm, inner),
        (left_hbm, left),
        (right_hbm, right),
        (mix_t_hbm, mix_t),
    )
    copies = [pltpu.make_async_copy(a, b, sems.at[i]) for i, (a, b) in enumerate(pairs)]
    for copy in copies:
        copy.start()
    copies[0].wait()
    copies[1].wait()
    lane_half = ((iota((1, ROWS), 1) >> 2) & 1).astype(f32).astype(bf16)
    upper_mix = mix[...] * lane_half
    both = jnp.concatenate([mix[...] - upper_mix, upper_mix], axis=0)
    halves = dot(both, rows[...]).astype(bf16)
    mixed = jnp.concatenate([halves[:SLOTS], halves[SLOTS:]], axis=1)
    copies[2].wait()
    before = dot(mixed, weight[...])
    erf = 0.5 * (1.0 + lax.erf(before * ROOT_HALF))
    acted = (before * erf).astype(bf16)
    acts[...] = acted
    act_copies = [
        pltpu.make_async_copy(acts.at[pl.ds(i * TILE, TILE), :], to, act_sems.at[i])
        for i, to in enumerate((top_hbm, bottom_hbm))
    ]
    for copy in act_copies:
        copy.start()
    slope = erf + before * (INV_ROOT_TAU * jnp.exp(-0.5 * before * before))
    for copy in copies[3:6]:
        copy.wait()
    rims = jnp.concatenate([left[...], right[...]], axis=0).astype(f32)
    grad_before = ((inner[...] + rims) * slope).astype(bf16)
    grad_mix = dot_t(grad_before, weight[...]).astype(bf16)
    copies[6].wait()
    send_rows(
        lambda r: interleave(dot(mix_t[r, :], grad_mix[:, :HALF]), dot(mix_t[r, :], grad_mix[:, HALF:])),
        out,
        out_hbm,
        out_sems,
    )
    for copy in act_copies:
        copy.wait()


def middle(*arrays):
    return pl.pallas_call(
        middle_kernel,
        out_shape=(
            jax.ShapeDtypeStruct((TILE, D), bf16),
            jax.ShapeDtypeStruct((TILE, D), bf16),
            jax.ShapeDtypeStruct((ROWS, HALF), bf16),
        ),
        in_specs=[ANY] * 7,
        out_specs=(ANY,) * 3,
        scratch_shapes=[pltpu.VMEM((SLOTS, D), bf16), pltpu.VMEM((ROWS, HALF), bf16)]
        + [pltpu.VMEM(a.shape, a.dtype) for a in arrays]
        + [pltpu.SemaphoreType.DMA((n,)) for n in (7, 2, PIECES)],
        compiler_params=params(63.9),
        cost_estimate=cost(3 * 10**9, 8 * 2**20),
        name="middle",
    )(*arrays)


def own_part_kernel(
    top_hbm, bottom_hbm, band_hbm, part_ref, first_ref, last_ref, acts, band, sems
):
    copies = [
        pltpu.make_async_copy(top_hbm, acts.at[pl.ds(0, TILE), :], sems.at[0]),
        pltpu.make_async_copy(bottom_hbm, acts.at[pl.ds(TILE, TILE), :], sems.at[1]),
        pltpu.make_async_copy(band_hbm, band, sems.at[2]),
    ]
    for copy in copies:
        copy.start()
    for copy in copies:
        copy.wait()
    part_ref[...] = dot(band[:, TILE : TILE + SLOTS], acts[...])
    first_ref[...] = band[:, :TILE]
    last_ref[...] = band[:, TILE + SLOTS :]


def own_part(*arrays):
    return pl.pallas_call(
        own_part_kernel,
        out_shape=(
            jax.ShapeDtypeStruct((SLOTS, D), f32),
            jax.ShapeDtypeStruct((SLOTS, TILE), bf16),
            jax.ShapeDtypeStruct((SLOTS, TILE), bf16),
        ),
        in_specs=[ANY] * 3,
        out_specs=(VMEM,) * 3,
        scratch_shapes=[
            pltpu.VMEM((SLOTS, D), bf16),
            pltpu.VMEM((SLOTS, 2 * SLOTS), bf16),
            pltpu.SemaphoreType.DMA((3,)),
        ],
        compiler_params=params(16),
        cost_estimate=cost(2 * 10**8, 3 * 2**20),
        name="own_part",
    )(*arrays)


def finish_kernel(part_ref, first_ref, last_ref, left_ref, right_ref, weight_ref, out_ref):
    mixed = part_ref[...] + dot(first_ref[...], left_ref[...]) + dot(last_ref[...], right_ref[...])
    out_ref[...] = dot(mixed.astype(bf16), weight_ref[...]).astype(bf16)


def finish(*arrays):
    return pl.pallas_call(
        finish_kernel,
        out_shape=jax.ShapeDtypeStruct((SLOTS, D), bf16),
        in_specs=[VMEM] * 6,
        out_specs=VMEM,
        compiler_params=params(16),
        cost_estimate=cost(10**9, 5 * 2**20),
        name="finish",
    )(*arrays)


def gather_kernel(target_ref, rows_ref, out_ref, pick):
    diagonal = iota((NODES, NPAD), 0) == iota((NODES, NPAD), 1)
    own_row = jnp.sum(jnp.where(diagonal, target_ref[0:1, :], 0), axis=1, keepdims=True)
    halo_row = jnp.sum(jnp.where(diagonal, target_ref[1:2, :], 0), axis=1, keepdims=True)
    lanes = iota((NODES, ROWS), 1)
    for u in range(2):
        hit = (lanes == own_row + 4 * u) | (lanes == halo_row + 4 * u)
        pick[u * NODES : (u + 1) * NODES, :] = jnp.where(hit, 1.0, 0.0).astype(bf16)
    picked = dot(pick[...], rows_ref[...]).astype(bf16)
    out_ref[:, :HALF] = picked[:NODES]
    out_ref[:, HALF:] = picked[NODES:]


def gather(target, rows):
    return pl.pallas_call(
        gather_kernel,
        out_shape=jax.ShapeDtypeStruct((NODES, D), bf16),
        in_specs=[VMEM, VMEM],
        out_specs=VMEM,
        scratch_shapes=[pltpu.VMEM((2 * NODES, ROWS), bf16)],
        compiler_params=params(16),
        cost_estimate=cost(4 * 10**8, 2 * 2**20),
        name="gather",
    )(target, rows)


def swap(rows):
    return lax.all_to_all(
        rows.reshape(PEERS, 8, HALF), ("enc", "dom"), split_axis=0, concat_axis=0, tiled=True
    ).reshape(ROWS, HALF)


def local(
    token_states,
    token_nodes,
    expand_weight,
    contract_weight,
    node_owner,
    tile_columns,
    tile_count,
    tile_values,
    first_weight,
    second_weight,
    output_cotangent,
):
    device = lax.axis_index("enc") * GROUP + lax.axis_index("dom")
    upper = (device >= PEERS // 2).astype(jnp.int32).reshape(1)
    rightward = [(i, i + 1) for i in range(GROUP - 1)]
    leftward = [(i + 1, i) for i in range(GROUP - 1)]
    outgoing, target = encode(
        upper, node_owner.reshape(1, NODES), token_nodes, token_states, expand_weight, contract_weight
    )
    arrived = swap(outgoing)
    target, later_cotangent = lax.optimization_barrier((target, output_cotangent))
    low, high, inner = spread(tile_columns, tile_count, tile_values, later_cotangent, second_weight)
    mix, mix_t, band = prepare(tile_columns, tile_count, tile_values, inner)
    from_right = lax.ppermute(low, "dom", leftward)
    from_left = lax.ppermute(high, "dom", rightward)
    top, bottom, grads = middle(arrived, mix, first_weight, inner, from_left, from_right, mix_t)
    returned = swap(grads)
    left = lax.ppermute(bottom, "dom", rightward)
    right = lax.ppermute(top, "dom", leftward)
    part, first, last = own_part(top, bottom, band)
    graph_output = finish(part, first, last, left, right, second_weight)
    return (graph_output, gather(target, returned))


def solution(mesh):
    rows = ("enc", "dom")
    placed = (
        P(rows, None),
        P(rows, None),
        P(),
        P(),
        P(rows, None),
        P(rows, None, None),
        P(rows, None),
        P(rows, None, None, None, None),
        P(),
        P(),
        P(rows, None),
    )
    return jax.shard_map(
        local,
        mesh=mesh,
        in_specs=placed,
        out_specs=(P(rows, None), P(rows, None)),
        check_vma=False,
    )
```
